32 devices in a mesh: dom: 8 (over z, y), cls: 4 (over x, core).
Axes of the slice: x: 2, y: 2, z: 4, core: 2. Of those that a mesh axis runs over, the one named last changes fastest.
Arguments:
- particles: bfloat16 [512, 2, 36, 128], P('dom'), may hold values from -16 to 16
- references: bfloat16 [48, 2, 36, 128], P('cls', None, None, 'dom'), may hold values from -8 to 8
- noise_weights: float32 [128], replicated, may hold values from 0.005 to 0.2
Outputs:
- class_spectra: float32 [48, 2, 36, 128], P('cls', None, None, 'dom')
- log_evidence: float32 [512], P('dom')
The draws below stay inside these ranges and needn't reach their ends.
All inputs are finite; a program needn't handle non-finite values.
Results may differ from the reference program's by a relative error of at most 0.035.
Values may be sent and summed in bfloat16 or wider, within the bound.
A program may use at most 64 MiB of HBM per device.

```python
import jax
import jax.numpy as jnp
from jax import lax

CYCLES = 128
ANGLES = 36
SHIFTS = 5
PART_DEV = 64
CLASSES = 48
PARTICLES = 512
N_DOM = 8


def class_draw(key, spread):
    normals = jnp.clip(jax.random.normal(key, (CLASSES, 2, ANGLES, CYCLES), jnp.float32), -5.0, 5.0)
    factor = jax.random.uniform(jax.random.fold_in(key, 11), (CLASSES, 1, 1, 1), jnp.float32, -1.0, 1.0)
    scales = jnp.exp(spread * factor)
    scales = scales.at[0:2].set(1.0)
    classes_drawn = normals * scales
    blended = classes_drawn[1]
    return classes_drawn.at[1].set(blended)


def draw_references(key, part):
    drawn = class_draw(key, 0.0)
    return drawn.astype(jnp.bfloat16)


def place_aligned(drawn, normals, classes_drawn, mean_weight):
    norm_guess = 2.0 * ANGLES * CYCLES * mean_weight
    amplitude = min(40.0, 0.5 + 300.0 / norm_guess)
    for number in range(3):
        strength = amplitude * (1.0 - 0.15 * number)
        aligned = strength * jnp.roll(classes_drawn[0], 5 * number + 3, axis=1)
        aligned = aligned + 0.1 * normals[number * PART_DEV]
        drawn = drawn.at[number * PART_DEV].set(aligned)
    return drawn


def draw_particles(key, part):
    classes_drawn = class_draw(key, 0.0)
    key = jax.random.fold_in(key, 3)
    normals = jnp.clip(jax.random.normal(key, (PARTICLES, 2, ANGLES, CYCLES), jnp.float32), -5.0, 5.0)
    drawn = place_aligned(normals, normals, classes_drawn, 0.0284)
    return jnp.clip(drawn, -16.0, 16.0).astype(jnp.bfloat16)


def draw_noise_weights(key, part):
    key = jax.random.fold_in(key, 5)
    position = jnp.arange(CYCLES, dtype=jnp.float32) / CYCLES
    jitter = jnp.exp(jax.random.uniform(key, (CYCLES,), jnp.float32, -0.5, 0.5))
    drawn = 0.015 * 3.0 ** position * jitter
    return drawn


def setup_inputs(seed: int = 0) -> dict:
    keys = jax.random.split(jax.random.key(seed), 4)
    return {
        "particles": draw_particles(jax.random.fold_in(keys[3], 71), 0),
        "references": draw_references(jax.random.fold_in(keys[3], 71), 0),
        "noise_weights": draw_noise_weights(jax.random.fold_in(keys[3], 71), 0),
    }


ridge_term = 0.5
shift_x = (0.0, 1.0, -1.0, 0.0, 0.0)
shift_y = (0.0, 0.0, 0.0, 1.0, -1.0)


def rounded(values):
    return lax.optimization_barrier(values.astype(jnp.bfloat16)).astype(jnp.float32)


def phase_tables(angles, cycles, shift_index):
    theta = 2.0 * jnp.pi * jnp.arange(angles, dtype=jnp.float32) / angles
    radius = jnp.arange(cycles, dtype=jnp.float32) / (2.0 * cycles)
    along = shift_x[shift_index] * jnp.cos(theta) + shift_y[shift_index] * jnp.sin(theta)
    phase = -2.0 * jnp.pi * along[:, None] * radius[None, :]
    return jnp.cos(phase), jnp.sin(phase)


def rotation_tables(angles):
    steps = jnp.arange(angles, dtype=jnp.int32)
    product = (steps[:, None] * steps[None, :]) % angles
    turn = 2.0 * jnp.pi * product.astype(jnp.float32) / angles
    return jnp.cos(turn), jnp.sin(turn)


def angular_table(angles):
    cosine, sine = rotation_tables(angles)
    upper = jnp.stack([cosine, -sine], axis=1)
    lower = jnp.stack([sine, cosine], axis=1)
    return jnp.stack([upper, lower], axis=0).astype(jnp.bfloat16)


def shifted_spectra(block, shift_index, table):
    cosine, sine = phase_tables(block.shape[2], block.shape[3], shift_index)
    real_part = block[:, 0].astype(jnp.float32)
    imag_part = block[:, 1].astype(jnp.float32)
    shifted = jnp.stack([real_part * cosine - imag_part * sine, real_part * sine + imag_part * cosine], axis=1)
    shifted = rounded(shifted)
    spectra = jnp.einsum("npar,paqm->nqmr", shifted, table.astype(jnp.float32))
    return rounded(spectra)


def reference(particles, references, noise_weights):
    angles = ANGLES
    cycles = CYCLES
    table = angular_table(angles)
    cosine_k, sine_k = rotation_tables(angles)
    whole = references.astype(jnp.float32)
    ref_spectra = jnp.einsum("cpar,paqm->cqmr", whole, table.astype(jnp.float32))
    weighted = rounded(noise_weights * ref_spectra)
    class_norms = jnp.sum(noise_weights * whole * whole, axis=(1, 2, 3))
    stacked = jnp.concatenate([weighted, jnp.stack([-weighted[:, 1], weighted[:, 0]], axis=1)], axis=0)
    classes = class_norms.shape[0]
    blocks = particles.reshape(N_DOM, PART_DEV, 2, angles, cycles)

    def one_block(carry, block):
        sums, denominators = carry
        spectra_list = []
        score_list = []
        for shift_index in range(SHIFTS):
            spectra = shifted_spectra(block, shift_index, table)
            spectra_list.append(spectra)
            correlation = jnp.einsum("nqmr,dqmr->mnd", spectra, stacked)
            real_correlation = correlation[:, :, :classes]
            imag_correlation = correlation[:, :, classes:]
            score = (jnp.einsum("mnc,mk->nck", real_correlation, cosine_k, precision=lax.Precision.HIGHEST)
                     - jnp.einsum("mnc,mk->nck", imag_correlation, sine_k, precision=lax.Precision.HIGHEST)) / angles
            score_list.append(score - 0.5 * class_norms[None, :, None])
        scores = jnp.stack(score_list, axis=2)
        peaks = jnp.max(scores, axis=(1, 2, 3))
        expo = jnp.exp(scores - peaks[:, None, None, None])
        totals = jnp.sum(expo, axis=(1, 2, 3))
        posterior = expo / totals[:, None, None, None]
        evidence = peaks + jnp.log(totals)
        block_sums = jnp.zeros((classes, 2, angles, cycles), jnp.float32)
        for shift_index in range(SHIFTS):
            chosen = posterior[:, :, shift_index, :]
            real_weight = rounded(jnp.einsum("nck,mk->ncm", chosen, cosine_k, precision=lax.Precision.HIGHEST))
            imag_weight = rounded(jnp.einsum("nck,mk->ncm", chosen, sine_k, precision=lax.Precision.HIGHEST))
            both = jnp.stack([real_weight, imag_weight], axis=1)
            parts = jnp.einsum("npcm,nqmr->pqcmr", both, spectra_list[shift_index])
            real_sum = parts[0, 0] - parts[1, 1]
            imag_sum = parts[0, 1] + parts[1, 0]
            block_sums = block_sums + jnp.stack([real_sum, imag_sum], axis=1)
        block_weights = jnp.sum(posterior, axis=(0, 2, 3))
        block_denominators = noise_weights[None, :] * block_weights[:, None]
        sums = sums + rounded(block_sums)
        denominators = denominators + rounded(block_denominators)
        return (sums, denominators), evidence

    start = (jnp.zeros((classes, 2, angles, cycles), jnp.float32), jnp.zeros((classes, cycles), jnp.float32))
    (sums, denominators), evidence = lax.scan(one_block, start, blocks)
    class_spectra = noise_weights * sums / (denominators[:, None, None, :] + ridge_term)
    return class_spectra, evidence.reshape(PARTICLES)
```

```python
import functools

import jax
import jax.numpy as jnp
from jax import lax
from jax.experimental import pallas as pl
from jax.experimental.pallas import tpu as pltpu
from jax.sharding import PartitionSpec as P

SHIFTS = 5
MESH = pl.DeviceIdType.MESH

ridge_term = 0.5
shift_x = (0.0, 1.0, -1.0, 0.0, 0.0)
shift_y = (0.0, 0.0, 0.0, 1.0, -1.0)


def phase_tables(angles, cycles, shift_index):
    theta = 2.0 * jnp.pi * jnp.arange(angles, dtype=jnp.float32) / angles
    radius = jnp.arange(cycles, dtype=jnp.float32) / (2.0 * cycles)
    along = shift_x[shift_index] * jnp.cos(theta) + shift_y[shift_index] * jnp.sin(theta)
    phase = -2.0 * jnp.pi * along[:, None] * radius[None, :]
    return (jnp.cos(phase), jnp.sin(phase))


def rotation_tables(angles):
    steps = jnp.arange(angles, dtype=jnp.int32)
    product = steps[:, None] * steps[None, :] % angles
    turn = 2.0 * jnp.pi * product.astype(jnp.float32) / angles
    return (jnp.cos(turn), jnp.sin(turn))


def angular_table(angles):
    cosine, sine = rotation_tables(angles)
    upper = jnp.stack([cosine, -sine], axis=1)
    lower = jnp.stack([sine, cosine], axis=1)
    return jnp.stack([upper, lower], axis=0).astype(jnp.bfloat16)


def greet(axis, count):
    me = lax.axis_index(axis)
    barrier = pltpu.get_barrier_semaphore()
    for step in range(1, count):
        pl.semaphore_signal(
            barrier,
            inc=1,
            device_id={axis: lax.rem(me + step, count)},
            device_id_type=MESH,
        )
    pl.semaphore_wait(barrier, count - 1)
    return me


def push(axis, count, me, source, land, send_sem, recv_sem):
    copies = []
    for step in range(1, count):
        peer = lax.rem(me + step, count)
        copy = pltpu.make_async_remote_copy(
            src_ref=source(peer),
            dst_ref=land.at[me],
            send_sem=send_sem.at[step],
            recv_sem=recv_sem.at[step],
            device_id={axis: peer},
            device_id_type=MESH,
        )
        copy.start()
        copies.append(copy)
    return copies


def gather_kernel(axis, count, x_ref, o_ref, land, send_sem, recv_sem):
    me = greet(axis, count)
    copies = push(axis, count, me, lambda peer: x_ref, land, send_sem, recv_sem)
    land[me] = x_ref[...]
    for copy in copies:
        copy.wait()
    o_ref[...] = land[...]


def gather(axis, count, identity, x):
    return pl.pallas_call(
        functools.partial(gather_kernel, axis, count),
        out_shape=jax.ShapeDtypeStruct((count,) + x.shape, x.dtype),
        in_specs=[pl.BlockSpec(memory_space=pltpu.VMEM)],
        out_specs=pl.BlockSpec(memory_space=pltpu.VMEM),
        scratch_shapes=[
            pltpu.VMEM((count,) + x.shape, x.dtype),
            pltpu.SemaphoreType.DMA((count,)),
            pltpu.SemaphoreType.DMA((count,)),
        ],
        compiler_params=pltpu.CompilerParams(collective_id=identity, has_side_effects=True),
    )(x)


def scatter_kernel(
    axis, count, x_ref, t_ref, o_ref, u_ref, land, t_land, send_sem, recv_sem, t_send, t_recv
):
    me = greet(axis, count)
    copies = push(axis, count, me, lambda peer: x_ref.at[peer], land, send_sem, recv_sem)
    copies += push(axis, count, me, lambda peer: t_ref, t_land, t_send, t_recv)
    land[me] = x_ref[me]
    t_land[me] = t_ref[...]
    for copy in copies:
        copy.wait()
    total = land[0].astype(jnp.float32)
    weight = t_land[0]
    for index in range(1, count):
        total = total + land[index].astype(jnp.float32)
        weight = weight + t_land[index]
    o_ref[...] = total
    u_ref[...] = weight


def scatter(axis, count, identity, x, t):
    return pl.pallas_call(
        functools.partial(scatter_kernel, axis, count),
        out_shape=(
            jax.ShapeDtypeStruct(x.shape[1:], jnp.float32),
            jax.ShapeDtypeStruct(t.shape, jnp.float32),
        ),
        in_specs=[pl.BlockSpec(memory_space=pltpu.VMEM)] * 2,
        out_specs=(pl.BlockSpec(memory_space=pltpu.VMEM),) * 2,
        scratch_shapes=[
            pltpu.VMEM(x.shape, x.dtype),
            pltpu.VMEM((count,) + t.shape, t.dtype),
            pltpu.SemaphoreType.DMA((count,)),
            pltpu.SemaphoreType.DMA((count,)),
            pltpu.SemaphoreType.DMA((count,)),
            pltpu.SemaphoreType.DMA((count,)),
        ],
        compiler_params=pltpu.CompilerParams(collective_id=identity, has_side_effects=True),
    )(x, t)


def posterior_kernel(axis, count, x_ref, o_ref, e_ref, mine, land, send_sem, recv_sem):
    me = greet(axis, count)
    peak = jnp.max(x_ref[...], axis=1, keepdims=True)
    expo = jnp.exp(x_ref[...] - peak)
    o_ref[...] = expo
    total = jnp.sum(expo, axis=1, keepdims=True)
    lanes = lax.broadcasted_iota(jnp.int32, mine.shape, 1)
    mine[...] = jnp.where(lanes == 0, peak, total)
    copies = push(axis, count, me, lambda peer: mine, land, send_sem, recv_sem)
    land[me] = mine[...]
    for copy in copies:
        copy.wait()
    peaks = land[0][:, 0:1]
    for index in range(1, count):
        peaks = jnp.maximum(peaks, land[index][:, 0:1])
    totals = jnp.zeros_like(peaks)
    for index in range(count):
        part = land[index]
        totals = totals + part[:, 1:2] * jnp.exp(part[:, 0:1] - peaks)
    o_ref[...] = o_ref[...] * (jnp.exp(peak - peaks) / totals)
    e_ref[...] = jnp.broadcast_to(peaks + jnp.log(totals), e_ref.shape)


def posteriors(axis, count, identity, x):
    rows = x.shape[0]
    return pl.pallas_call(
        functools.partial(posterior_kernel, axis, count),
        out_shape=(
            jax.ShapeDtypeStruct(x.shape, jnp.float32),
            jax.ShapeDtypeStruct((rows, 128), jnp.float32),
        ),
        in_specs=[pl.BlockSpec(memory_space=pltpu.VMEM)],
        out_specs=(pl.BlockSpec(memory_space=pltpu.VMEM),) * 2,
        scratch_shapes=[
            pltpu.VMEM((rows, 128), jnp.float32),
            pltpu.VMEM((count, rows, 128), jnp.float32),
            pltpu.SemaphoreType.DMA((count,)),
            pltpu.SemaphoreType.DMA((count,)),
        ],
        compiler_params=pltpu.CompilerParams(collective_id=identity, has_side_effects=True),
    )(x)


def per_device(dom, cls, particles, references, noise_weights):
    particle_count, _, angles, cycles = particles.shape
    classes = references.shape[0]
    cycle_count = cycles // dom
    rows = -(-cycle_count // 16) * 16
    wide = classes * 2 * angles
    table = angular_table(angles)
    cosine_k, sine_k = rotation_tables(angles)

    own = references.reshape(wide, cycle_count).T
    own = jnp.pad(own, ((0, rows - cycle_count), (0, 0)))
    whole = gather("dom", dom, 0, own)[:, :cycle_count].reshape(cycles, classes, 2, angles)
    whole_wide = whole.astype(jnp.float32)
    ref_spectra = jnp.einsum("rcpa,paqm->mqrc", whole, table, preferred_element_type=jnp.float32)
    weighted = (noise_weights[None, None, :, None] * ref_spectra).astype(jnp.bfloat16)
    class_norms = jnp.sum(noise_weights[:, None, None, None] * whole_wide * whole_wide, axis=(0, 2, 3))
    stacked = jnp.concatenate(
        [weighted, jnp.stack([-weighted[:, 1], weighted[:, 0]], axis=1)], axis=3
    )

    spectra_list = []
    for shift_index in range(SHIFTS):
        cosine, sine = phase_tables(angles, cycles, shift_index)
        real_part = particles[:, 0].astype(jnp.float32)
        imag_part = particles[:, 1].astype(jnp.float32)
        shifted = jnp.stack(
            [real_part * cosine - imag_part * sine, real_part * sine + imag_part * cosine], axis=1
        ).astype(jnp.bfloat16)
        spectra_list.append(
            jnp.einsum(
                "npar,paqm->mnqr", shifted, table, preferred_element_type=jnp.float32
            ).astype(jnp.bfloat16)
        )
    spectra = jnp.stack(spectra_list, axis=1)
    correlation = jnp.einsum("msnqr,mqrd->snmd", spectra, stacked, preferred_element_type=jnp.float32)
    turn = jnp.stack([cosine_k, -sine_k], axis=1) / angles
    both_parts = correlation.reshape(SHIFTS, particle_count, angles, 2, classes)
    scores = jnp.einsum("snmpc,mpk->nsck", both_parts, turn, precision=lax.Precision.HIGHEST)
    scores = scores - 0.5 * class_norms[None, None, :, None]
    posterior, evidence = posteriors("cls", cls, 1, scores.reshape(particle_count, -1))
    posterior = posterior.reshape(particle_count, SHIFTS, classes, angles)

    back = jnp.stack([cosine_k, sine_k], axis=0)
    both = jnp.einsum(
        "nsck,pmk->mpcsn", posterior, back, precision=lax.Precision.HIGHEST
    ).astype(jnp.bfloat16)
    parts = jnp.einsum("mpcsn,msnqr->mpcqr", both, spectra, preferred_element_type=jnp.float32)
    real_sum = parts[:, 0, :, 0] - parts[:, 1, :, 1]
    imag_sum = parts[:, 0, :, 1] + parts[:, 1, :, 0]
    sums = jnp.stack([real_sum, imag_sum], axis=2).astype(jnp.bfloat16)
    sums = jnp.transpose(sums, (3, 1, 2, 0)).reshape(dom, cycle_count, wide)
    sums = jnp.pad(sums, ((0, 0), (0, rows - cycle_count), (0, 0)))
    weight_sums = jnp.sum(posterior, axis=(0, 1, 3))
    weight_block = jnp.broadcast_to(weight_sums[None, :], (8, classes))
    own_sums, own_weights = scatter("dom", dom, 2, sums, weight_block)
    own_sums = own_sums[:cycle_count].T.reshape(classes, 2, angles, cycle_count)
    cycle_start = lax.axis_index("dom") * cycle_count
    noise = lax.dynamic_slice_in_dim(noise_weights, cycle_start, cycle_count, 0)
    denominator = noise * own_weights[0][:, None] + ridge_term
    class_spectra = own_sums * (noise / denominator)[:, None, None, :]
    return (class_spectra, evidence[:, 0])


def solution(mesh):
    dom, cls = mesh.shape["dom"], mesh.shape["cls"]
    return jax.shard_map(
        functools.partial(per_device, dom, cls),
        mesh=mesh,
        in_specs=(P("dom", None, None, None), P("cls", None, None, "dom"), P()),
        out_specs=(P("cls", None, None, "dom"), P("dom")),
        check_vma=False,
    )
```

```python
import functools

import jax
import jax.numpy as jnp
import ml_dtypes
import numpy as np
from jax import lax
from jax.experimental import pallas as pl
from jax.experimental.pallas import tpu as pltpu
from jax.sharding import PartitionSpec as P

SHIFTS = 5
MESH = pl.DeviceIdType.MESH

ridge_term = 0.5
shift_x = (0.0, 1.0, -1.0, 0.0, 0.0)
shift_y = (0.0, 0.0, 0.0, 1.0, -1.0)


def rotation_tables(angles):
    steps = jnp.arange(angles, dtype=jnp.int32)
    product = steps[:, None] * steps[None, :] % angles
    turn = 2.0 * jnp.pi * product.astype(jnp.float32) / angles
    return (jnp.cos(turn), jnp.sin(turn))


def angular_table(angles):
    cosine, sine = rotation_tables(angles)
    upper = jnp.stack([cosine, -sine], axis=1)
    lower = jnp.stack([sine, cosine], axis=1)
    return jnp.stack([upper, lower], axis=0).astype(jnp.bfloat16)


def greet(axis, count):
    me = lax.axis_index(axis)
    barrier = pltpu.get_barrier_semaphore()
    for step in range(1, count):
        pl.semaphore_signal(
            barrier,
            inc=1,
            device_id={axis: lax.rem(me + step, count)},
            device_id_type=MESH,
        )
    pl.semaphore_wait(barrier, count - 1)
    return me


def push(axis, count, me, source, land, send_sem, recv_sem):
    copies = []
    for step in range(1, count):
        peer = lax.rem(me + step, count)
        copy = pltpu.make_async_remote_copy(
            src_ref=source(peer),
            dst_ref=land.at[me],
            send_sem=send_sem.at[step],
            recv_sem=recv_sem.at[step],
            device_id={axis: peer},
            device_id_type=MESH,
        )
        copy.start()
        copies.append(copy)
    return copies


def phase_constants(angles, cycles):
    theta = (2.0 * np.pi * np.arange(angles) / angles).astype(np.float32)
    radius = (np.arange(cycles) / (2.0 * cycles)).astype(np.float32)
    straight, crossed = [], []
    for dx, dy in zip(shift_x, shift_y):
        along = dx * np.cos(theta) + dy * np.sin(theta)
        phase = -2.0 * np.pi * along[:, None] * radius[None, :]
        cosine, sine = np.cos(phase), np.sin(phase)
        straight.append(np.concatenate([cosine, cosine], axis=1))
        crossed.append(np.concatenate([-sine, sine], axis=1))
    return np.stack(straight).astype(np.float32), np.stack(crossed).astype(np.float32)


def odd_factor(count):
    return count // 4


def rounded_root(index, count):
    turn = 2.0 * np.pi * (index % count) / count
    cosine, sine = np.float32(np.cos(turn)), np.float32(np.sin(turn))
    return float(cosine.astype(ml_dtypes.bfloat16)), float(sine.astype(ml_dtypes.bfloat16))


def swapped(z):
    half = z.shape[-1] // 2
    return jnp.concatenate([z[..., half:], z[..., :half]], axis=-1)


def turned(z):
    half = z.shape[-1] // 2
    return jnp.concatenate([z[..., half:], -z[..., :half]], axis=-1)


def transform(load, middle, store, angles):
    odd = odd_factor(angles)
    inverse = pow(4, -1, odd)
    quarter = pow(odd, -1, 4)
    for second in range(odd):
        z = [load((odd * first + 4 * second) % angles) for first in range(4)]
        plus, minus = z[0] + z[2], z[0] - z[2]
        other, differ = z[1] + z[3], turned(z[1] - z[3])
        middle[0, second] = plus + other
        middle[1, second] = minus + differ
        middle[2, second] = plus - other
        middle[3, second] = minus - differ
    for first in range(4):
        head = middle[first, 0]
        pairs = odd // 2
        even, uneven = [], []
        for j in range(1, pairs + 1):
            low, high = middle[first, j], middle[first, odd - j]
            even.append(low + high)
            uneven.append(turned(low - high))
        total = head
        for part in even:
            total = total + part
        store((odd * quarter * first) % angles, total)
        for k in range(1, pairs + 1):
            real, imag = head, None
            for j in range(1, pairs + 1):
                cosine, sine = rounded_root(k * j, odd)
                real = real + cosine * even[j - 1]
                term = sine * uneven[j - 1]
                imag = term if imag is None else imag + term
            base = odd * quarter * first
            store((base + 4 * inverse * k) % angles, real + imag)
            store((base + 4 * inverse * (odd - k)) % angles, real - imag)


TILE = 16


def spectra_kernel(
    axis, count, w_ref, x_ref, c_ref, s_ref, o_ref, g_ref, land, middle, send_sem, recv_sem
):
    me = greet(axis, count)
    copies = push(axis, count, me, lambda peer: w_ref, land, send_sem, recv_sem)
    land[me] = w_ref[...]
    angles, particle_count = x_ref.shape[0], x_ref.shape[1]
    tiles = particle_count // TILE

    def step(index, carry):
        shift = index // tiles
        start = pl.multiple_of(lax.rem(index, tiles) * TILE, TILE)
        target = pl.multiple_of(index * TILE, TILE)

        def load(angle):
            z = x_ref[angle, pl.ds(start, TILE), :].astype(jnp.float32)
            straight = c_ref[shift, pl.ds(angle, 1), :]
            crossed = s_ref[shift, pl.ds(angle, 1), :]
            return z * straight + swapped(z) * crossed

        def store(frequency, value):
            o_ref[frequency, pl.ds(target, TILE), :] = value.astype(o_ref.dtype)

        transform(load, middle, store, angles)
        return carry

    lax.fori_loop(0, SHIFTS * tiles, step, 0)
    for copy in copies:
        copy.wait()
    g_ref[...] = land[...]


def spectra_and_gather(axis, count, identity, w, x, straight, crossed):
    angles, particle_count, wide = x.shape
    return pl.pallas_call(
        functools.partial(spectra_kernel, axis, count),
        out_shape=(
            jax.ShapeDtypeStruct((angles, SHIFTS * particle_count, wide), jnp.bfloat16),
            jax.ShapeDtypeStruct((count,) + w.shape, w.dtype),
        ),
        in_specs=[pl.BlockSpec(memory_space=pltpu.VMEM)] * 4,
        out_specs=(pl.BlockSpec(memory_space=pltpu.VMEM),) * 2,
        scratch_shapes=[
            pltpu.VMEM((count,) + w.shape, w.dtype),
            pltpu.VMEM((4, odd_factor(angles), TILE, wide), jnp.float32),
            pltpu.SemaphoreType.DMA((count,)),
            pltpu.SemaphoreType.DMA((count,)),
        ],
        compiler_params=pltpu.CompilerParams(
            collective_id=identity, has_side_effects=True, vmem_limit_bytes=40 * 1024 * 1024
        ),
    )(w, x, straight, crossed)


def scatter_kernel(
    axis, count, x_ref, t_ref, o_ref, u_ref, land, t_land, send_sem, recv_sem, t_send, t_recv
):
    me = greet(axis, count)
    copies = push(axis, count, me, lambda peer: x_ref.at[peer], land, send_sem, recv_sem)
    copies += push(axis, count, me, lambda peer: t_ref, t_land, t_send, t_recv)
    land[me] = x_ref[me]
    t_land[me] = t_ref[...]
    for copy in copies:
        copy.wait()
    total = land[0].astype(jnp.float32)
    weight = t_land[0]
    for index in range(1, count):
        total = total + land[index].astype(jnp.float32)
        weight = weight + t_land[index]
    o_ref[...] = total
    u_ref[...] = weight


def scatter(axis, count, identity, x, t):
    return pl.pallas_call(
        functools.partial(scatter_kernel, axis, count),
        out_shape=(
            jax.ShapeDtypeStruct(x.shape[1:], jnp.float32),
            jax.ShapeDtypeStruct(t.shape, jnp.float32),
        ),
        in_specs=[pl.BlockSpec(memory_space=pltpu.VMEM)] * 2,
        out_specs=(pl.BlockSpec(memory_space=pltpu.VMEM),) * 2,
        scratch_shapes=[
            pltpu.VMEM(x.shape, x.dtype),
            pltpu.VMEM((count,) + t.shape, t.dtype),
            pltpu.SemaphoreType.DMA((count,)),
            pltpu.SemaphoreType.DMA((count,)),
            pltpu.SemaphoreType.DMA((count,)),
            pltpu.SemaphoreType.DMA((count,)),
        ],
        compiler_params=pltpu.CompilerParams(collective_id=identity, has_side_effects=True),
    )(x, t)


def posterior_kernel(axis, count, x_ref, o_ref, e_ref, mine, land, send_sem, recv_sem):
    me = greet(axis, count)
    peak = jnp.max(x_ref[...], axis=1, keepdims=True)
    expo = jnp.exp(x_ref[...] - peak)
    o_ref[...] = expo
    total = jnp.sum(expo, axis=1, keepdims=True)
    lanes = lax.broadcasted_iota(jnp.int32, mine.shape, 1)
    mine[...] = jnp.where(lanes == 0, peak, total)
    copies = push(axis, count, me, lambda peer: mine, land, send_sem, recv_sem)
    land[me] = mine[...]
    for copy in copies:
        copy.wait()
    peaks = land[0][:, 0:1]
    for index in range(1, count):
        peaks = jnp.maximum(peaks, land[index][:, 0:1])
    totals = jnp.zeros_like(peaks)
    for index in range(count):
        part = land[index]
        totals = totals + part[:, 1:2] * jnp.exp(part[:, 0:1] - peaks)
    o_ref[...] = o_ref[...] * (jnp.exp(peak - peaks) / totals)
    e_ref[...] = jnp.broadcast_to(peaks + jnp.log(totals), e_ref.shape)


def posteriors(axis, count, identity, x):
    rows = x.shape[0]
    return pl.pallas_call(
        functools.partial(posterior_kernel, axis, count),
        out_shape=(
            jax.ShapeDtypeStruct(x.shape, jnp.float32),
            jax.ShapeDtypeStruct((rows, 128), jnp.float32),
        ),
        in_specs=[pl.BlockSpec(memory_space=pltpu.VMEM)],
        out_specs=(pl.BlockSpec(memory_space=pltpu.VMEM),) * 2,
        scratch_shapes=[
            pltpu.VMEM((rows, 128), jnp.float32),
            pltpu.VMEM((count, rows, 128), jnp.float32),
            pltpu.SemaphoreType.DMA((count,)),
            pltpu.SemaphoreType.DMA((count,)),
        ],
        compiler_params=pltpu.CompilerParams(collective_id=identity, has_side_effects=True),
    )(x)


def per_device(dom, cls, particles, references, noise_weights):
    particle_count, _, angles, cycles = particles.shape
    classes = references.shape[0]
    cycle_count = cycles // dom
    rows = -(-cycle_count // 16) * 16
    wide = classes * 2 * angles
    table = angular_table(angles)
    cosine_k, sine_k = rotation_tables(angles)

    own = references.reshape(wide, cycle_count).T
    own = jnp.pad(own, ((0, rows - cycle_count), (0, 0)))
    arranged = jnp.transpose(particles, (2, 0, 1, 3)).reshape(angles, particle_count, 2 * cycles)
    straight, crossed = phase_constants(angles, cycles)
    spectra, whole = spectra_and_gather("dom", dom, 0, own, arranged, straight, crossed)
    spectra = spectra.reshape(angles, SHIFTS, particle_count, 2, cycles)
    whole = whole[:, :cycle_count].reshape(cycles, classes, 2, angles)
    whole_wide = whole.astype(jnp.float32)
    ref_spectra = jnp.einsum("rcpa,paqm->mqrc", whole, table, preferred_element_type=jnp.float32)
    weighted = (noise_weights[None, None, :, None] * ref_spectra).astype(jnp.bfloat16)
    class_norms = jnp.sum(noise_weights[:, None, None, None] * whole_wide * whole_wide, axis=(0, 2, 3))
    stacked = jnp.concatenate(
        [weighted, jnp.stack([-weighted[:, 1], weighted[:, 0]], axis=1)], axis=3
    )

    correlation = jnp.einsum("msnqr,mqrd->snmd", spectra, stacked, preferred_element_type=jnp.float32)
    turn = jnp.stack([cosine_k, -sine_k], axis=1) / angles
    both_parts = correlation.reshape(SHIFTS, particle_count, angles, 2, classes)
    scores = jnp.einsum("snmpc,mpk->nsck", both_parts, turn, precision=lax.Precision.HIGHEST)
    scores = scores - 0.5 * class_norms[None, None, :, None]
    posterior, evidence = posteriors("cls", cls, 1, scores.reshape(particle_count, -1))
    posterior = posterior.reshape(particle_count, SHIFTS, classes, angles)

    back = jnp.stack([cosine_k, sine_k], axis=0)
    both = jnp.einsum(
        "nsck,pmk->mpcsn", posterior, back, precision=lax.Precision.HIGHEST
    ).astype(jnp.bfloat16)
    parts = jnp.einsum("mpcsn,msnqr->mpcqr", both, spectra, preferred_element_type=jnp.float32)
    real_sum = parts[:, 0, :, 0] - parts[:, 1, :, 1]
    imag_sum = parts[:, 0, :, 1] + parts[:, 1, :, 0]
    sums = jnp.stack([real_sum, imag_sum], axis=2).astype(jnp.bfloat16)
    sums = jnp.transpose(sums, (3, 1, 2, 0)).reshape(dom, cycle_count, wide)
    sums = jnp.pad(sums, ((0, 0), (0, rows - cycle_count), (0, 0)))
    weight_sums = jnp.sum(posterior, axis=(0, 1, 3))
    weight_block = jnp.broadcast_to(weight_sums[None, :], (8, classes))
    own_sums, own_weights = scatter("dom", dom, 2, sums, weight_block)
    own_sums = own_sums[:cycle_count].T.reshape(classes, 2, angles, cycle_count)
    cycle_start = lax.axis_index("dom") * cycle_count
    noise = lax.dynamic_slice_in_dim(noise_weights, cycle_start, cycle_count, 0)
    denominator = noise * own_weights[0][:, None] + ridge_term
    class_spectra = own_sums * (noise / denominator)[:, None, None, :]
    return (class_spectra, evidence[:, 0])


def solution(mesh):
    dom, cls = mesh.shape["dom"], mesh.shape["cls"]
    return jax.shard_map(
        functools.partial(per_device, dom, cls),
        mesh=mesh,
        in_specs=(P("dom", None, None, None), P("cls", None, None, "dom"), P()),
        out_specs=(P("cls", None, None, "dom"), P("dom")),
        check_vma=False,
    )
```

```python
import functools

import jax
import jax.numpy as jnp
import ml_dtypes
import numpy as np
from jax import lax
from jax.experimental import pallas as pl
from jax.experimental.pallas import tpu as pltpu
from jax.sharding import PartitionSpec as P

SHIFTS = 5
MESH = pl.DeviceIdType.MESH

ridge_term = 0.5
shift_x = (0.0, 1.0, -1.0, 0.0, 0.0)
shift_y = (0.0, 0.0, 0.0, 1.0, -1.0)


def rotation_tables(angles):
    steps = jnp.arange(angles, dtype=jnp.int32)
    product = steps[:, None] * steps[None, :] % angles
    turn = 2.0 * jnp.pi * product.astype(jnp.float32) / angles
    return (jnp.cos(turn), jnp.sin(turn))


def angular_table(angles):
    cosine, sine = rotation_tables(angles)
    upper = jnp.stack([cosine, -sine], axis=1)
    lower = jnp.stack([sine, cosine], axis=1)
    return jnp.stack([upper, lower], axis=0).astype(jnp.bfloat16)


def greet(counts):
    barrier = pltpu.get_barrier_semaphore()
    for axis, count in counts.items():
        me = lax.axis_index(axis)
        for step in range(1, count):
            pl.semaphore_signal(
                barrier,
                inc=1,
                device_id={axis: lax.rem(me + step, count)},
                device_id_type=MESH,
            )
    pl.semaphore_wait(barrier, sum(counts.values()) - len(counts))


def push(axis, count, me, source, land, send_sem, recv_sem):
    copies = []
    for step in range(1, count):
        peer = lax.rem(me + step, count)
        copy = pltpu.make_async_remote_copy(
            src_ref=source(peer),
            dst_ref=land.at[me],
            send_sem=send_sem.at[step],
            recv_sem=recv_sem.at[step],
            device_id={axis: peer},
            device_id_type=MESH,
        )
        copy.start()
        copies.append(copy)
    return copies


def phase_constants(angles, cycles):
    theta = (2.0 * np.pi * np.arange(angles) / angles).astype(np.float32)
    radius = (np.arange(cycles) / (2.0 * cycles)).astype(np.float32)
    straight, crossed = [], []
    for dx, dy in zip(shift_x, shift_y):
        along = dx * np.cos(theta) + dy * np.sin(theta)
        phase = -2.0 * np.pi * along[:, None] * radius[None, :]
        cosine, sine = np.cos(phase), np.sin(phase)
        straight.append(np.concatenate([cosine, cosine], axis=1))
        crossed.append(np.concatenate([-sine, sine], axis=1))
    return np.stack(straight).astype(np.float32), np.stack(crossed).astype(np.float32)


def odd_factor(count):
    return count // 4


def full_root(index, count):
    turn = 2.0 * np.pi * (index % count) / count
    return float(np.cos(turn)), float(np.sin(turn))


def rounded_root(index, count):
    turn = 2.0 * np.pi * (index % count) / count
    cosine, sine = np.float32(np.cos(turn)), np.float32(np.sin(turn))
    return float(cosine.astype(ml_dtypes.bfloat16)), float(sine.astype(ml_dtypes.bfloat16))


def swapped(z):
    half = z.shape[-1] // 2
    return jnp.concatenate([z[..., half:], z[..., :half]], axis=-1)


def turned(z, axis):
    low, high = jnp.split(z, 2, axis=axis)
    return jnp.concatenate([high, -low], axis=axis)


def transform(load, middle, store, angles, root, axis):
    odd = odd_factor(angles)
    inverse = pow(4, -1, odd)
    quarter = pow(odd, -1, 4)
    for second in range(odd):
        z = [load((odd * first + 4 * second) % angles) for first in range(4)]
        plus, minus = z[0] + z[2], z[0] - z[2]
        other, differ = z[1] + z[3], turned(z[1] - z[3], axis)
        middle[0, second] = plus + other
        middle[1, second] = minus + differ
        middle[2, second] = plus - other
        middle[3, second] = minus - differ
    for first in range(4):
        head = middle[first, 0]
        pairs = odd // 2
        even, uneven = [], []
        for j in range(1, pairs + 1):
            low, high = middle[first, j], middle[first, odd - j]
            even.append(low + high)
            uneven.append(turned(low - high, axis))
        total = head
        for part in even:
            total = total + part
        store((odd * quarter * first) % angles, total)
        for k in range(1, pairs + 1):
            real, imag = head, None
            for j in range(1, pairs + 1):
                cosine, sine = root(k * j, odd)
                real = real + cosine * even[j - 1]
                term = sine * uneven[j - 1]
                imag = term if imag is None else imag + term
            base = odd * quarter * first
            store((base + 4 * inverse * k) % angles, real + imag)
            store((base + 4 * inverse * (odd - k)) % angles, real - imag)


TILE = 16
BLOCK = 128


def em_kernel(
    dom, cls, classes,
    w_ref, h_ref, x_ref, c_ref, s_ref,
    o_ref, u_ref, e_ref,
    spectra, w_land, h_land, turned_w, middle, corr, wide_middle, scores, weights,
    stat, stat_land, sums, outgoing, land, total_block, total_land,
    w_send, w_recv, h_send, h_recv, stat_send, stat_recv, o_send, o_recv, t_send, t_recv,
):
    greet({"dom": dom, "cls": cls})
    me, column = lax.axis_index("dom"), lax.axis_index("cls")
    copies = push("dom", dom, me, lambda peer: w_ref, w_land, w_send, w_recv)
    copies += push("dom", dom, me, lambda peer: h_ref, h_land, h_send, h_recv)
    w_land[me] = w_ref[...]
    h_land[me] = h_ref[...]
    angles, particle_count, width = x_ref.shape
    cycles = width // 2
    cycle_count = cycles // dom
    tiles = particle_count // TILE
    padded = scores.shape[1]
    pairs = 2 * classes

    def step(index, carry):
        shift = index // tiles
        start = pl.multiple_of(lax.rem(index, tiles) * TILE, TILE)
        target = pl.multiple_of(index * TILE, TILE)

        def load(angle):
            z = x_ref[angle, pl.ds(start, TILE), :].astype(jnp.float32)
            straight = c_ref[shift, pl.ds(angle, 1), :]
            crossed = s_ref[shift, pl.ds(angle, 1), :]
            return z * straight + swapped(z) * crossed

        def store(frequency, value):
            spectra[frequency, pl.ds(target, TILE), :] = value.astype(spectra.dtype)

        transform(load, middle, store, angles, rounded_root, 1)
        return carry

    lax.fori_loop(0, SHIFTS * tiles, step, 0)

    for copy in copies:
        copy.wait()
    half_norms = h_land[0]
    for index in range(1, dom):
        half_norms = half_norms + h_land[index]
    row = lax.broadcasted_iota(jnp.int32, half_norms.shape, 0)
    half_norms = jnp.where(row < classes, 0.5 * half_norms, 1e30)[:, 0:1]
    for block in range(turned_w.shape[0] // BLOCK):
        lanes = slice(block * BLOCK, (block + 1) * BLOCK)
        piece = jnp.concatenate(
            [w_land[index][:, lanes].astype(jnp.float32)[:cycle_count] for index in range(dom)], axis=0
        )
        turned_w[lanes, :] = piece.T

    def correlate(m, carry):
        both = turned_w[pl.ds(pl.multiple_of(m * pairs, 8), pairs), :]
        gap = jnp.zeros((padded - classes, cycles), jnp.float32)
        real = jnp.concatenate([both[:classes], gap], axis=0)
        imag = jnp.concatenate([both[classes:], gap], axis=0)
        left = jnp.concatenate([real, imag], axis=0)
        right = jnp.concatenate([imag, -real], axis=0)
        stacked = jnp.concatenate([left, right], axis=1).astype(jnp.bfloat16)
        corr[m] = lax.dot_general(
            stacked, spectra[m], (((1,), (1,)), ((), ())), preferred_element_type=jnp.float32
        )
        return carry

    lax.fori_loop(0, angles, correlate, 0)

    def keep_score(k, value):
        scores[k] = value[:padded] * (1.0 / angles) - half_norms

    transform(lambda m: corr[m], wide_middle, keep_score, angles, full_root, 0)

    def fold(values, combine):
        parts = [
            values[:, index * particle_count : (index + 1) * particle_count] for index in range(SHIFTS)
        ]
        return functools.reduce(combine, parts)

    def spread(values):
        return jnp.concatenate([values] * SHIFTS, axis=1)

    highest = lax.fori_loop(1, angles, lambda k, best: jnp.maximum(best, scores[k]), scores[0])
    peak = fold(jnp.max(highest, axis=0, keepdims=True), jnp.maximum)
    wide_peak = spread(peak)

    def exponentiate(k, total):
        value = jnp.exp(scores[k] - wide_peak)
        scores[k] = value
        return total + value

    class_total = lax.fori_loop(0, angles, exponentiate, jnp.zeros(scores.shape[1:], jnp.float32))
    total = fold(jnp.sum(class_total, axis=0, keepdims=True), jnp.add)
    row = lax.broadcasted_iota(jnp.int32, stat.shape, 0)
    stat[...] = jnp.where(row == 0, peak, total)
    copies = push("cls", cls, column, lambda peer: stat, stat_land, stat_send, stat_recv)
    stat_land[column] = stat[...]
    for copy in copies:
        copy.wait()
    peaks = stat_land[0][0:1]
    for index in range(1, cls):
        peaks = jnp.maximum(peaks, stat_land[index][0:1])
    totals = jnp.zeros_like(peaks)
    for index in range(cls):
        part = stat_land[index]
        totals = totals + part[1:2] * jnp.exp(part[0:1] - peaks)
    scale = spread(jnp.exp(peak - peaks) / totals)
    e_ref[...] = jnp.broadcast_to(peaks + jnp.log(totals), e_ref.shape)
    weight = jnp.sum(class_total * scale, axis=1, keepdims=True)
    total_block[...] = jnp.broadcast_to(weight, total_block.shape)
    copies = push("dom", dom, me, lambda peer: total_block, total_land, t_send, t_recv)
    total_land[me] = total_block[...]

    def load_posterior(k):
        value = scores[k] * scale
        return jnp.concatenate([value, jnp.zeros_like(value)], axis=0)

    def keep_weight(m, value):
        weights[m] = jnp.concatenate([value[:padded], -value[padded:]], axis=0).astype(weights.dtype)

    transform(load_posterior, wide_middle, keep_weight, angles, full_root, 0)

    used = angles * pairs
    if sums.shape[0] > used:
        sums[used:] = jnp.zeros((sums.shape[0] - used, cycles), jnp.float32)

    def accumulate(m, carry):
        parts = jnp.dot(weights[m], spectra[m], preferred_element_type=jnp.float32)
        real = parts[:padded, :cycles] - parts[padded:, cycles:]
        imag = parts[:padded, cycles:] + parts[padded:, :cycles]
        sums[pl.ds(pl.multiple_of(m * pairs, 8), pairs), :] = jnp.concatenate(
            [real[:classes], imag[:classes]], axis=0
        )
        return carry

    lax.fori_loop(0, angles, accumulate, 0)
    rows = outgoing.shape[1]
    for block in range(sums.shape[0] // BLOCK):
        lanes = slice(block * BLOCK, (block + 1) * BLOCK)
        piece = sums[lanes, :].T
        for index in range(dom):
            part = piece[index * cycle_count : (index + 1) * cycle_count]
            if rows > cycle_count:
                gap = jnp.zeros((rows - cycle_count, BLOCK), jnp.float32)
                part = jnp.concatenate([part, gap], axis=0)
            outgoing[index, :, lanes] = part.astype(outgoing.dtype)
    copies += push("dom", dom, me, lambda peer: outgoing.at[peer], land, o_send, o_recv)
    land[me] = outgoing[me]
    for copy in copies:
        copy.wait()
    result = land[0].astype(jnp.float32)
    weight = total_land[0]
    for index in range(1, dom):
        result = result + land[index].astype(jnp.float32)
        weight = weight + total_land[index]
    o_ref[...] = result
    u_ref[...] = weight


def em_step(dom, cls, classes, w, h, x, straight, crossed):
    angles, particle_count, width = x.shape
    cycles = width // 2
    rows, long = w.shape
    padded = h.shape[0]
    images = SHIFTS * particle_count
    odd = odd_factor(angles)
    f32, b16 = jnp.float32, jnp.bfloat16
    scratch = [
        pltpu.VMEM((angles, images, width), b16),
        pltpu.VMEM((dom, rows, long), b16),
        pltpu.VMEM((dom,) + h.shape, f32),
        pltpu.VMEM((long, cycles), f32),
        pltpu.VMEM((4, odd, TILE, width), f32),
        pltpu.VMEM((angles, 2 * padded, images), f32),
        pltpu.VMEM((4, odd, 2 * padded, images), f32),
        pltpu.VMEM((angles, padded, images), f32),
        pltpu.VMEM((angles, 2 * padded, images), b16),
        pltpu.VMEM((8, particle_count), f32),
        pltpu.VMEM((cls, 8, particle_count), f32),
        pltpu.VMEM((long, cycles), f32),
        pltpu.VMEM((dom, rows, long), b16),
        pltpu.VMEM((dom, rows, long), b16),
        pltpu.VMEM((padded, BLOCK), f32),
        pltpu.VMEM((dom, padded, BLOCK), f32),
    ]
    for count in (dom, dom, cls, dom, dom):
        scratch += [pltpu.SemaphoreType.DMA((count,))] * 2
    return pl.pallas_call(
        functools.partial(em_kernel, dom, cls, classes),
        out_shape=(
            jax.ShapeDtypeStruct((rows, long), f32),
            jax.ShapeDtypeStruct((padded, BLOCK), f32),
            jax.ShapeDtypeStruct((8, particle_count), f32),
        ),
        in_specs=[pl.BlockSpec(memory_space=pltpu.VMEM)] * 5,
        out_specs=(pl.BlockSpec(memory_space=pltpu.VMEM),) * 3,
        scratch_shapes=scratch,
        compiler_params=pltpu.CompilerParams(
            collective_id=0, has_side_effects=True, vmem_limit_bytes=40 * 1024 * 1024
        ),
    )(w, h, x, straight, crossed)


def per_device(dom, cls, particles, references, noise_weights):
    particle_count, _, angles, cycles = particles.shape
    classes = references.shape[0]
    cycle_count = cycles // dom
    rows = -(-cycle_count // 16) * 16
    padded = -(-classes // 8) * 8
    used = classes * 2 * angles
    long = -(-used // BLOCK) * BLOCK
    table = angular_table(angles)
    cycle_start = lax.axis_index("dom") * cycle_count
    noise = lax.dynamic_slice_in_dim(noise_weights, cycle_start, cycle_count, 0)

    ref_spectra = jnp.einsum(
        "cpar,paqm->rmqc", references, table, preferred_element_type=jnp.float32
    )
    weighted = (noise[:, None, None, None] * ref_spectra).astype(jnp.bfloat16)
    weighted = jnp.pad(
        weighted.reshape(cycle_count, used), ((0, rows - cycle_count), (0, long - used))
    )
    own_wide = references.astype(jnp.float32)
    norms = jnp.sum(noise * own_wide * own_wide, axis=(1, 2, 3))
    norms = jnp.broadcast_to(jnp.pad(norms, (0, padded - classes))[:, None], (padded, BLOCK))
    arranged = jnp.transpose(particles, (2, 0, 1, 3)).reshape(angles, particle_count, 2 * cycles)
    straight, crossed = phase_constants(angles, cycles)
    own_sums, own_weights, evidence = em_step(
        dom, cls, classes, weighted, norms, arranged, straight, crossed
    )
    own_sums = own_sums[:cycle_count, :used].reshape(cycle_count, angles, 2, classes)
    own_sums = jnp.transpose(own_sums, (3, 2, 1, 0))
    denominator = noise * own_weights[:classes, 0:1] + ridge_term
    class_spectra = own_sums * (noise / denominator)[:, None, None, :]
    return (class_spectra, evidence[0])


def solution(mesh):
    dom, cls = mesh.shape["dom"], mesh.shape["cls"]
    return jax.shard_map(
        functools.partial(per_device, dom, cls),
        mesh=mesh,
        in_specs=(P("dom", None, None, None), P("cls", None, None, "dom"), P()),
        out_specs=(P("cls", None, None, "dom"), P("dom")),
        check_vma=False,
    )
```

```python
import functools

import jax
import jax.numpy as jnp
import ml_dtypes
import numpy as np
from jax import lax
from jax.experimental import pallas as pl
from jax.experimental.pallas import tpu as pltpu
from jax.sharding import PartitionSpec as P

SHIFTS = 5
MESH = pl.DeviceIdType.MESH

ridge_term = 0.5
shift_x = (0.0, 1.0, -1.0, 0.0, 0.0)
shift_y = (0.0, 0.0, 0.0, 1.0, -1.0)


def rotation_tables(angles):
    steps = jnp.arange(angles, dtype=jnp.int32)
    product = steps[:, None] * steps[None, :] % angles
    turn = 2.0 * jnp.pi * product.astype(jnp.float32) / angles
    return (jnp.cos(turn), jnp.sin(turn))


def angular_table(angles):
    cosine, sine = rotation_tables(angles)
    upper = jnp.stack([cosine, -sine], axis=1)
    lower = jnp.stack([sine, cosine], axis=1)
    return jnp.stack([upper, lower], axis=0).astype(jnp.bfloat16)


def greet(counts):
    barrier = pltpu.get_barrier_semaphore()
    for axis, count in counts.items():
        me = lax.axis_index(axis)
        for step in range(1, count):
            pl.semaphore_signal(
                barrier,
                inc=1,
                device_id={axis: lax.rem(me + step, count)},
                device_id_type=MESH,
            )
    pl.semaphore_wait(barrier, sum(counts.values()) - len(counts))


def push(axis, count, me, source, land, send_sem, recv_sem, lanes=None):
    copies = []
    for step in range(1, count):
        peer = lax.rem(me + step, count)
        copy = pltpu.make_async_remote_copy(
            src_ref=source(peer),
            dst_ref=land.at[me] if lanes is None else land.at[me, :, lanes],
            send_sem=send_sem.at[step],
            recv_sem=recv_sem.at[step],
            device_id={axis: peer},
            device_id_type=MESH,
        )
        copy.start()
        copies.append(copy)
    return copies


def phase_constants(angles, cycles):
    theta = (2.0 * np.pi * np.arange(angles) / angles).astype(np.float32)
    radius = (np.arange(cycles) / (2.0 * cycles)).astype(np.float32)
    straight, crossed = [], []
    for dx, dy in zip(shift_x, shift_y):
        along = dx * np.cos(theta) + dy * np.sin(theta)
        phase = -2.0 * np.pi * along[:, None] * radius[None, :]
        cosine, sine = np.cos(phase), np.sin(phase)
        straight.append(np.concatenate([cosine, cosine], axis=1))
        crossed.append(np.concatenate([-sine, sine], axis=1))
    return np.stack(straight).astype(np.float32), np.stack(crossed).astype(np.float32)


def odd_factor(count):
    return count // 4


def full_root(index, count):
    turn = 2.0 * np.pi * (index % count) / count
    return float(np.cos(turn)), float(np.sin(turn))


def rounded_root(index, count):
    turn = 2.0 * np.pi * (index % count) / count
    cosine, sine = np.float32(np.cos(turn)), np.float32(np.sin(turn))
    return float(cosine.astype(ml_dtypes.bfloat16)), float(sine.astype(ml_dtypes.bfloat16))


def swapped(z):
    half = z.shape[-1] // 2
    return jnp.concatenate([z[..., half:], z[..., :half]], axis=-1)


def turned(z, axis):
    low, high = jnp.split(z, 2, axis=axis)
    return jnp.concatenate([high, -low], axis=axis)


def transform(load, middle, store, angles, root, axis):
    odd = odd_factor(angles)
    inverse = pow(4, -1, odd)
    quarter = pow(odd, -1, 4)
    for second in range(odd):
        z = [load((odd * first + 4 * second) % angles) for first in range(4)]
        plus, minus = z[0] + z[2], z[0] - z[2]
        other, differ = z[1] + z[3], turned(z[1] - z[3], axis)
        middle[0, second] = plus + other
        middle[1, second] = minus + differ
        middle[2, second] = plus - other
        middle[3, second] = minus - differ
    for first in range(4):
        head = middle[first, 0]
        pairs = odd // 2
        even, uneven = [], []
        for j in range(1, pairs + 1):
            low, high = middle[first, j], middle[first, odd - j]
            even.append(low + high)
            uneven.append(turned(low - high, axis))
        total = head
        for part in even:
            total = total + part
        store((odd * quarter * first) % angles, total)
        for k in range(1, pairs + 1):
            real, imag = head, None
            for j in range(1, pairs + 1):
                cosine, sine = root(k * j, odd)
                real = real + cosine * even[j - 1]
                term = sine * uneven[j - 1]
                imag = term if imag is None else imag + term
            base = odd * quarter * first
            store((base + 4 * inverse * k) % angles, real + imag)
            store((base + 4 * inverse * (odd - k)) % angles, real - imag)


TILE = 16
BLOCK = 128


def em_kernel(
    dom, cls, classes,
    w_ref, h_ref, x_ref, c_ref, s_ref,
    o_ref, u_ref, e_ref,
    spectra, w_land, h_land, turned_w, middle, corr, wide_middle, scores, weights,
    stat, stat_land, sums, outgoing, land, total_block, total_land,
    w_send, w_recv, h_send, h_recv, stat_send, stat_recv, o_send, o_recv, t_send, t_recv,
):
    greet({"dom": dom, "cls": cls})
    me, column = lax.axis_index("dom"), lax.axis_index("cls")
    copies = push("dom", dom, me, lambda peer: w_ref, w_land, w_send, w_recv)
    copies += push("dom", dom, me, lambda peer: h_ref, h_land, h_send, h_recv)
    w_land[me] = w_ref[...]
    h_land[me] = h_ref[...]
    angles, particle_count, width = x_ref.shape
    cycles = width // 2
    cycle_count = cycles // dom
    tiles = particle_count // TILE
    padded = scores.shape[1]
    pairs = 2 * classes

    def step(index, carry):
        shift = index // tiles
        start = pl.multiple_of(lax.rem(index, tiles) * TILE, TILE)
        target = pl.multiple_of(index * TILE, TILE)

        def load(angle):
            z = x_ref[angle, pl.ds(start, TILE), :].astype(jnp.float32)
            straight = c_ref[shift, pl.ds(angle, 1), :]
            crossed = s_ref[shift, pl.ds(angle, 1), :]
            return z * straight + swapped(z) * crossed

        def store(frequency, value):
            spectra[frequency, pl.ds(target, TILE), :] = value.astype(spectra.dtype)

        transform(load, middle, store, angles, rounded_root, 1)
        return carry

    lax.fori_loop(0, SHIFTS * tiles, step, 0)

    for copy in copies:
        copy.wait()
    half_norms = h_land[0]
    for index in range(1, dom):
        half_norms = half_norms + h_land[index]
    row = lax.broadcasted_iota(jnp.int32, half_norms.shape, 0)
    half_norms = jnp.where(row < classes, 0.5 * half_norms, 1e30)[:, 0:1]
    for block in range(turned_w.shape[0] // BLOCK):
        lanes = slice(block * BLOCK, (block + 1) * BLOCK)
        piece = jnp.concatenate(
            [w_land[index][:, lanes].astype(jnp.float32)[:cycle_count] for index in range(dom)], axis=0
        )
        turned_w[lanes, :] = piece.T

    def correlate(m, carry):
        both = turned_w[pl.ds(pl.multiple_of(m * pairs, 8), pairs), :]
        gap = jnp.zeros((padded - classes, cycles), jnp.float32)
        real = jnp.concatenate([both[:classes], gap], axis=0)
        imag = jnp.concatenate([both[classes:], gap], axis=0)
        left = jnp.concatenate([real, imag], axis=0)
        right = jnp.concatenate([imag, -real], axis=0)
        stacked = jnp.concatenate([left, right], axis=1).astype(jnp.bfloat16)
        corr[m] = lax.dot_general(
            stacked, spectra[m], (((1,), (1,)), ((), ())), preferred_element_type=jnp.float32
        )
        return carry

    lax.fori_loop(0, angles, correlate, 0, unroll=6)

    def keep_score(k, value):
        scores[k] = value[:padded] * (1.0 / angles) - half_norms

    transform(lambda m: corr[m], wide_middle, keep_score, angles, full_root, 0)

    def fold(values, combine):
        parts = [
            values[:, index * particle_count : (index + 1) * particle_count] for index in range(SHIFTS)
        ]
        return functools.reduce(combine, parts)

    def spread(values):
        return jnp.concatenate([values] * SHIFTS, axis=1)

    highest = scores[0]
    for k in range(1, angles):
        highest = jnp.maximum(highest, scores[k])
    peak = fold(jnp.max(highest, axis=0, keepdims=True), jnp.maximum)
    wide_peak = spread(peak)

    def exponentiate(k, total):
        value = jnp.exp(scores[k] - wide_peak)
        scores[k] = value
        return total + value

    empty = jnp.zeros(scores.shape[1:], jnp.float32)
    class_total = lax.fori_loop(0, angles, exponentiate, empty, unroll=6)
    total = fold(jnp.sum(class_total, axis=0, keepdims=True), jnp.add)
    row = lax.broadcasted_iota(jnp.int32, stat.shape, 0)
    stat[...] = jnp.where(row == 0, peak, total)
    copies = push("cls", cls, column, lambda peer: stat, stat_land, stat_send, stat_recv)
    stat_land[column] = stat[...]
    for copy in copies:
        copy.wait()
    peaks = stat_land[0][0:1]
    for index in range(1, cls):
        peaks = jnp.maximum(peaks, stat_land[index][0:1])
    totals = jnp.zeros_like(peaks)
    for index in range(cls):
        part = stat_land[index]
        totals = totals + part[1:2] * jnp.exp(part[0:1] - peaks)
    scale = spread(jnp.exp(peak - peaks) / totals)
    e_ref[...] = jnp.broadcast_to(peaks + jnp.log(totals), e_ref.shape)
    weight = jnp.sum(class_total * scale, axis=1, keepdims=True)
    total_block[...] = jnp.broadcast_to(weight, total_block.shape)
    copies = push("dom", dom, me, lambda peer: total_block, total_land, t_send, t_recv)
    total_land[me] = total_block[...]

    def load_posterior(k):
        value = scores[k] * scale
        return jnp.concatenate([value, jnp.zeros_like(value)], axis=0)

    def keep_weight(m, value):
        weights[m] = jnp.concatenate([value[:padded], -value[padded:]], axis=0).astype(weights.dtype)

    transform(load_posterior, wide_middle, keep_weight, angles, full_root, 0)

    used = angles * pairs
    if sums.shape[0] > used:
        sums[used:] = jnp.zeros((sums.shape[0] - used, cycles), jnp.float32)

    def accumulate(m, carry):
        parts = jnp.dot(weights[m], spectra[m], preferred_element_type=jnp.float32)
        real = parts[:padded, :cycles] - parts[padded:, cycles:]
        imag = parts[:padded, cycles:] + parts[padded:, :cycles]
        sums[pl.ds(pl.multiple_of(m * pairs, 8), pairs), :] = jnp.concatenate(
            [real[:classes], imag[:classes]], axis=0
        )
        return carry

    rows, blocks = outgoing.shape[1], sums.shape[0] // BLOCK
    split = (blocks + 1) // 2
    ready = min(angles, -(-split * BLOCK // pairs))
    for part, (first, last, head, tail) in enumerate(
        ((0, ready, 0, split), (ready, angles, split, blocks))
    ):
        lax.fori_loop(first, last, accumulate, 0, unroll=6)
        for block in range(head, tail):
            lanes = slice(block * BLOCK, (block + 1) * BLOCK)
            piece = sums[lanes, :].T
            for index in range(dom):
                own = piece[index * cycle_count : (index + 1) * cycle_count]
                if rows > cycle_count:
                    gap = jnp.zeros((rows - cycle_count, BLOCK), jnp.float32)
                    own = jnp.concatenate([own, gap], axis=0)
                outgoing[index, :, lanes] = own.astype(outgoing.dtype)
        lanes = slice(head * BLOCK, tail * BLOCK)
        copies += push(
            "dom", dom, me, lambda peer: outgoing.at[peer, :, lanes], land,
            o_send.at[part], o_recv.at[part], lanes,
        )
    land[me] = outgoing[me]
    for copy in copies:
        copy.wait()
    result = land[0].astype(jnp.float32)
    weight = total_land[0]
    for index in range(1, dom):
        result = result + land[index].astype(jnp.float32)
        weight = weight + total_land[index]
    o_ref[...] = result
    u_ref[...] = weight


def em_step(dom, cls, classes, w, h, x, straight, crossed):
    angles, particle_count, width = x.shape
    cycles = width // 2
    rows, long = w.shape
    padded = h.shape[0]
    images = SHIFTS * particle_count
    odd = odd_factor(angles)
    f32, b16 = jnp.float32, jnp.bfloat16
    scratch = [
        pltpu.VMEM((angles, images, width), b16),
        pltpu.VMEM((dom, rows, long), b16),
        pltpu.VMEM((dom,) + h.shape, f32),
        pltpu.VMEM((long, cycles), f32),
        pltpu.VMEM((4, odd, TILE, width), f32),
        pltpu.VMEM((angles, 2 * padded, images), f32),
        pltpu.VMEM((4, odd, 2 * padded, images), f32),
        pltpu.VMEM((angles, padded, images), f32),
        pltpu.VMEM((angles, 2 * padded, images), b16),
        pltpu.VMEM((8, particle_count), f32),
        pltpu.VMEM((cls, 8, particle_count), f32),
        pltpu.VMEM((long, cycles), f32),
        pltpu.VMEM((dom, rows, long), b16),
        pltpu.VMEM((dom, rows, long), b16),
        pltpu.VMEM((padded, BLOCK), f32),
        pltpu.VMEM((dom, padded, BLOCK), f32),
    ]
    for shape in ((dom,), (dom,), (cls,), (2, dom), (dom,)):
        scratch += [pltpu.SemaphoreType.DMA(shape)] * 2
    return pl.pallas_call(
        functools.partial(em_kernel, dom, cls, classes),
        out_shape=(
            jax.ShapeDtypeStruct((rows, long), f32),
            jax.ShapeDtypeStruct((padded, BLOCK), f32),
            jax.ShapeDtypeStruct((8, particle_count), f32),
        ),
        in_specs=[pl.BlockSpec(memory_space=pltpu.VMEM)] * 5,
        out_specs=(pl.BlockSpec(memory_space=pltpu.VMEM),) * 3,
        scratch_shapes=scratch,
        compiler_params=pltpu.CompilerParams(
            collective_id=0, has_side_effects=True, vmem_limit_bytes=40 * 1024 * 1024
        ),
    )(w, h, x, straight, crossed)


def per_device(dom, cls, particles, references, noise_weights):
    particle_count, _, angles, cycles = particles.shape
    classes = references.shape[0]
    cycle_count = cycles // dom
    rows = -(-cycle_count // 16) * 16
    padded = -(-classes // 8) * 8
    used = classes * 2 * angles
    long = -(-used // BLOCK) * BLOCK
    table = angular_table(angles)
    mine = jnp.arange(dom)[:, None] == lax.axis_index("dom")
    noise = jnp.sum(jnp.where(mine, noise_weights.reshape(dom, cycle_count), 0.0), axis=0)

    ref_spectra = jnp.einsum(
        "cpar,paqm->rmqc", references, table, preferred_element_type=jnp.float32
    )
    weighted = (noise[:, None, None, None] * ref_spectra).astype(jnp.bfloat16)
    weighted = jnp.pad(
        weighted.reshape(cycle_count, used), ((0, rows - cycle_count), (0, long - used))
    )
    own_wide = references.astype(jnp.float32)
    norms = jnp.sum(noise * own_wide * own_wide, axis=(1, 2, 3))
    norms = jnp.broadcast_to(jnp.pad(norms, (0, padded - classes))[:, None], (padded, BLOCK))
    arranged = jnp.transpose(particles, (2, 0, 1, 3)).reshape(angles, particle_count, 2 * cycles)
    straight, crossed = phase_constants(angles, cycles)
    own_sums, own_weights, evidence = em_step(
        dom, cls, classes, weighted, norms, arranged, straight, crossed
    )
    own_sums = own_sums[:cycle_count, :used].reshape(cycle_count, angles, 2, classes)
    own_sums = jnp.transpose(own_sums, (3, 2, 1, 0))
    denominator = noise * own_weights[:classes, 0:1] + ridge_term
    class_spectra = own_sums * (noise / denominator)[:, None, None, :]
    return (class_spectra, evidence[0])


def solution(mesh):
    dom, cls = mesh.shape["dom"], mesh.shape["cls"]
    return jax.shard_map(
        functools.partial(per_device, dom, cls),
        mesh=mesh,
        in_specs=(P("dom", None, None, None), P("cls", None, None, "dom"), P()),
        out_specs=(P("cls", None, None, "dom"), P("dom")),
        check_vma=False,
    )
```

```python
import functools

import jax
import jax.numpy as jnp
import ml_dtypes
import numpy as np
from jax import lax
from jax.experimental import pallas as pl
from jax.experimental.pallas import tpu as pltpu
from jax.sharding import PartitionSpec as P

SHIFTS = 5
MESH = pl.DeviceIdType.MESH

ridge_term = 0.5
shift_x = (0.0, 1.0, -1.0, 0.0, 0.0)
shift_y = (0.0, 0.0, 0.0, 1.0, -1.0)


def rotation_tables(angles):
    steps = jnp.arange(angles, dtype=jnp.int32)
    product = steps[:, None] * steps[None, :] % angles
    turn = 2.0 * jnp.pi * product.astype(jnp.float32) / angles
    return (jnp.cos(turn), jnp.sin(turn))


def angular_table(angles):
    cosine, sine = rotation_tables(angles)
    upper = jnp.stack([cosine, -sine], axis=1)
    lower = jnp.stack([sine, cosine], axis=1)
    return jnp.stack([upper, lower], axis=0).astype(jnp.bfloat16)


def greet(counts):
    barrier = pltpu.get_barrier_semaphore()
    for axis, count in counts.items():
        me = lax.axis_index(axis)
        for step in range(1, count):
            pl.semaphore_signal(
                barrier,
                inc=1,
                device_id={axis: lax.rem(me + step, count)},
                device_id_type=MESH,
            )
    pl.semaphore_wait(barrier, sum(counts.values()) - len(counts))


def push(axis, count, me, source, land, send_sem, recv_sem, lanes=None):
    copies = []
    for step in range(1, count):
        peer = lax.rem(me + step, count)
        copy = pltpu.make_async_remote_copy(
            src_ref=source(peer),
            dst_ref=land.at[me] if lanes is None else land.at[me, :, lanes],
            send_sem=send_sem.at[step],
            recv_sem=recv_sem.at[step],
            device_id={axis: peer},
            device_id_type=MESH,
        )
        copy.start()
        copies.append(copy)
    return copies


def phase_constants(angles, cycles):
    theta = (2.0 * np.pi * np.arange(angles) / angles).astype(np.float32)
    radius = (np.arange(cycles) / (2.0 * cycles)).astype(np.float32)
    straight, crossed = [], []
    for dx, dy in zip(shift_x, shift_y):
        along = dx * np.cos(theta) + dy * np.sin(theta)
        phase = -2.0 * np.pi * along[:, None] * radius[None, :]
        cosine, sine = np.cos(phase), np.sin(phase)
        straight.append(np.concatenate([cosine, cosine], axis=1))
        crossed.append(np.concatenate([-sine, sine], axis=1))
    return np.stack(straight).astype(np.float32), np.stack(crossed).astype(np.float32)


def odd_factor(count):
    return count // 4


def full_root(index, count):
    turn = 2.0 * np.pi * (index % count) / count
    return float(np.cos(turn)), float(np.sin(turn))


def rounded_root(index, count):
    turn = 2.0 * np.pi * (index % count) / count
    cosine, sine = np.float32(np.cos(turn)), np.float32(np.sin(turn))
    return float(cosine.astype(ml_dtypes.bfloat16)), float(sine.astype(ml_dtypes.bfloat16))


def swapped(z):
    half = z.shape[-1] // 2
    return jnp.concatenate([z[..., half:], z[..., :half]], axis=-1)


def turned(z, axis):
    low, high = jnp.split(z, 2, axis=axis)
    return jnp.concatenate([high, -low], axis=axis)


def transform(load, middle, store, angles, root, axis):
    odd = odd_factor(angles)
    inverse = pow(4, -1, odd)
    quarter = pow(odd, -1, 4)
    for second in range(odd):
        z = [load((odd * first + 4 * second) % angles) for first in range(4)]
        plus, minus = z[0] + z[2], z[0] - z[2]
        other, differ = z[1] + z[3], turned(z[1] - z[3], axis)
        middle[0, second] = plus + other
        middle[1, second] = minus + differ
        middle[2, second] = plus - other
        middle[3, second] = minus - differ
    for first in range(4):
        head = middle[first, 0]
        pairs = odd // 2
        even, uneven = [], []
        for j in range(1, pairs + 1):
            low, high = middle[first, j], middle[first, odd - j]
            even.append(low + high)
            uneven.append(turned(low - high, axis))
        total = head
        for part in even:
            total = total + part
        store((odd * quarter * first) % angles, total)
        products = {}

        def scaled(kind, parts, j, factor):
            if (kind, j, factor) not in products:
                products[kind, j, factor] = factor * parts[j - 1]
            return products[kind, j, factor]

        def weigh(kind, parts, terms):
            groups = {}
            for j, factor, sign in terms:
                groups.setdefault(factor, []).append((j, sign))
            total = None
            for factor, members in groups.items():
                if factor == 0.0:
                    continue
                if len(members) == 1:
                    j, sign = members[0]
                    part = parts[j - 1] if factor == 1.0 else scaled(kind, parts, j, factor)
                else:
                    j, sign = members[0]
                    part = parts[j - 1]
                    for other, turn in members[1:]:
                        value = parts[other - 1]
                        part = part + value if turn == sign else part - value
                    part = factor * part
                if total is None:
                    total = part if sign > 0 else -part
                else:
                    total = total + part if sign > 0 else total - part
            return total

        for k in range(1, pairs + 1):
            cosines, sines = [], []
            for j in range(1, pairs + 1):
                place = (k * j) % odd
                cosine, sine = root(min(place, odd - place), odd)
                cosines.append((j, abs(cosine), 1 if cosine >= 0.0 else -1))
                sines.append((j, sine, 1 if place <= pairs else -1))
            real = head + weigh("even", even, cosines)
            imag = weigh("uneven", uneven, sines)
            base = odd * quarter * first
            store((base + 4 * inverse * k) % angles, real + imag)
            store((base + 4 * inverse * (odd - k)) % angles, real - imag)


TILE = 16
BLOCK = 128


def em_kernel(
    dom, cls, classes,
    w_ref, h_ref, x_ref, c_ref, s_ref,
    o_ref, u_ref, e_ref,
    spectra, w_land, h_land, turned_w, middle, corr, wide_middle, scores, weights,
    stat, stat_land, sums, outgoing, land, total_block, total_land,
    w_send, w_recv, h_send, h_recv, stat_send, stat_recv, o_send, o_recv, t_send, t_recv,
):
    greet({"dom": dom, "cls": cls})
    me, column = lax.axis_index("dom"), lax.axis_index("cls")
    copies = push("dom", dom, me, lambda peer: w_ref, w_land, w_send, w_recv)
    copies += push("dom", dom, me, lambda peer: h_ref, h_land, h_send, h_recv)
    w_land[me] = w_ref[...]
    h_land[me] = h_ref[...]
    angles, particle_count, width = x_ref.shape
    cycles = width // 2
    cycle_count = cycles // dom
    tiles = particle_count // TILE
    padded = scores.shape[1]
    pairs = 2 * classes

    def step(index, carry):
        shift = index // tiles
        start = pl.multiple_of(lax.rem(index, tiles) * TILE, TILE)
        target = pl.multiple_of(index * TILE, TILE)

        def load(angle):
            z = x_ref[angle, pl.ds(start, TILE), :].astype(jnp.float32)
            straight = c_ref[shift, pl.ds(angle, 1), :]
            crossed = s_ref[shift, pl.ds(angle, 1), :]
            return z * straight + swapped(z) * crossed

        def store(frequency, value):
            spectra[frequency, pl.ds(target, TILE), :] = value.astype(spectra.dtype)

        transform(load, middle, store, angles, rounded_root, 1)
        return carry

    lax.fori_loop(0, SHIFTS * tiles, step, 0)

    for copy in copies:
        copy.wait()
    half_norms = h_land[0]
    for index in range(1, dom):
        half_norms = half_norms + h_land[index]
    row = lax.broadcasted_iota(jnp.int32, half_norms.shape, 0)
    half_norms = jnp.where(row < classes, 0.5 * half_norms, 1e30)[:, 0:1]
    for block in range(turned_w.shape[0] // BLOCK):
        lanes = slice(block * BLOCK, (block + 1) * BLOCK)
        piece = jnp.concatenate(
            [w_land[index][:, lanes].astype(jnp.float32)[:cycle_count] for index in range(dom)], axis=0
        )
        turned_w[lanes, :] = piece.T

    def correlate(m, carry):
        both = turned_w[pl.ds(pl.multiple_of(m * pairs, 8), pairs), :]
        gap = jnp.zeros((padded - classes, cycles), jnp.float32)
        real = jnp.concatenate([both[:classes], gap], axis=0)
        imag = jnp.concatenate([both[classes:], gap], axis=0)
        left = jnp.concatenate([real, imag], axis=0)
        right = jnp.concatenate([imag, -real], axis=0)
        stacked = jnp.concatenate([left, right], axis=1).astype(jnp.bfloat16)
        corr[m] = lax.dot_general(
            stacked, spectra[m], (((1,), (1,)), ((), ())), preferred_element_type=jnp.float32
        )
        return carry

    lax.fori_loop(0, angles, correlate, 0, unroll=6)

    images = SHIFTS * particle_count
    pieces = [slice(start, min(start + BLOCK, images)) for start in range(0, images, BLOCK)]

    def score_piece(lanes):
        def keep_score(k, value):
            scores[k, :, lanes] = value[:padded] * (1.0 / angles) - half_norms

        middle_piece = wide_middle.at[:, :, :, lanes]
        transform(lambda m: corr[m, :, lanes], middle_piece, keep_score, angles, full_root, 0)

    for lanes in pieces:
        score_piece(lanes)

    def fold(values, combine):
        parts = [
            values[:, index * particle_count : (index + 1) * particle_count] for index in range(SHIFTS)
        ]
        return functools.reduce(combine, parts)

    def spread(values):
        return jnp.concatenate([values] * SHIFTS, axis=1)

    highest = scores[0]
    for k in range(1, angles):
        highest = jnp.maximum(highest, scores[k])
    peak = fold(jnp.max(highest, axis=0, keepdims=True), jnp.maximum)
    wide_peak = spread(peak)

    def exponentiate(k, total):
        value = jnp.exp(scores[k] - wide_peak)
        scores[k] = value
        return total + value

    empty = jnp.zeros(scores.shape[1:], jnp.float32)
    class_total = lax.fori_loop(0, angles, exponentiate, empty, unroll=6)
    total = fold(jnp.sum(class_total, axis=0, keepdims=True), jnp.add)
    row = lax.broadcasted_iota(jnp.int32, stat.shape, 0)
    stat[...] = jnp.where(row == 0, peak, total)
    copies = push("cls", cls, column, lambda peer: stat, stat_land, stat_send, stat_recv)
    stat_land[column] = stat[...]
    for copy in copies:
        copy.wait()
    peaks = stat_land[0][0:1]
    for index in range(1, cls):
        peaks = jnp.maximum(peaks, stat_land[index][0:1])
    totals = jnp.zeros_like(peaks)
    for index in range(cls):
        part = stat_land[index]
        totals = totals + part[1:2] * jnp.exp(part[0:1] - peaks)
    scale = spread(jnp.exp(peak - peaks) / totals)
    e_ref[...] = jnp.broadcast_to(peaks + jnp.log(totals), e_ref.shape)
    weight = jnp.sum(class_total * scale, axis=1, keepdims=True)
    total_block[...] = jnp.broadcast_to(weight, total_block.shape)
    copies = push("dom", dom, me, lambda peer: total_block, total_land, t_send, t_recv)
    total_land[me] = total_block[...]

    def weight_piece(lanes):
        def load_posterior(k):
            value = scores[k, :, lanes] * scale[:, lanes]
            return jnp.concatenate([value, jnp.zeros_like(value)], axis=0)

        def keep_weight(m, value):
            both = jnp.concatenate([value[:padded], -value[padded:]], axis=0)
            weights[m, :, lanes] = both.astype(weights.dtype)

        middle_piece = wide_middle.at[:, :, :, lanes]
        transform(load_posterior, middle_piece, keep_weight, angles, full_root, 0)

    for lanes in pieces:
        weight_piece(lanes)

    used = angles * pairs
    if sums.shape[0] > used:
        sums[used:] = jnp.zeros((sums.shape[0] - used, cycles), jnp.float32)

    def accumulate(m, carry):
        parts = jnp.dot(weights[m], spectra[m], preferred_element_type=jnp.float32)
        real = parts[:padded, :cycles] - parts[padded:, cycles:]
        imag = parts[:padded, cycles:] + parts[padded:, :cycles]
        sums[pl.ds(pl.multiple_of(m * pairs, 8), pairs), :] = jnp.concatenate(
            [real[:classes], imag[:classes]], axis=0
        )
        return carry

    rows, blocks = outgoing.shape[1], sums.shape[0] // BLOCK
    split = (blocks + 1) // 2
    ready = min(angles, -(-split * BLOCK // pairs))
    for part, (first, last, head, tail) in enumerate(
        ((0, ready, 0, split), (ready, angles, split, blocks))
    ):
        lax.fori_loop(first, last, accumulate, 0, unroll=6)
        for block in range(head, tail):
            lanes = slice(block * BLOCK, (block + 1) * BLOCK)
            piece = sums[lanes, :].T
            for index in range(dom):
                own = piece[index * cycle_count : (index + 1) * cycle_count]
                if rows > cycle_count:
                    gap = jnp.zeros((rows - cycle_count, BLOCK), jnp.float32)
                    own = jnp.concatenate([own, gap], axis=0)
                outgoing[index, :, lanes] = own.astype(outgoing.dtype)
        lanes = slice(head * BLOCK, tail * BLOCK)
        copies += push(
            "dom", dom, me, lambda peer: outgoing.at[peer, :, lanes], land,
            o_send.at[part], o_recv.at[part], lanes,
        )
    land[me] = outgoing[me]
    for copy in copies:
        copy.wait()
    result = land[0].astype(jnp.float32)
    weight = total_land[0]
    for index in range(1, dom):
        result = result + land[index].astype(jnp.float32)
        weight = weight + total_land[index]
    o_ref[...] = result
    u_ref[...] = weight


def em_step(dom, cls, classes, w, h, x, straight, crossed):
    angles, particle_count, width = x.shape
    cycles = width // 2
    rows, long = w.shape
    padded = h.shape[0]
    images = SHIFTS * particle_count
    odd = odd_factor(angles)
    f32, b16 = jnp.float32, jnp.bfloat16
    scratch = [
        pltpu.VMEM((angles, images, width), b16),
        pltpu.VMEM((dom, rows, long), b16),
        pltpu.VMEM((dom,) + h.shape, f32),
        pltpu.VMEM((long, cycles), f32),
        pltpu.VMEM((4, odd, TILE, width), f32),
        pltpu.VMEM((angles, 2 * padded, images), f32),
        pltpu.VMEM((4, odd, 2 * padded, images), f32),
        pltpu.VMEM((angles, padded, images), f32),
        pltpu.VMEM((angles, 2 * padded, images), b16),
        pltpu.VMEM((8, particle_count), f32),
        pltpu.VMEM((cls, 8, particle_count), f32),
        pltpu.VMEM((long, cycles), f32),
        pltpu.VMEM((dom, rows, long), b16),
        pltpu.VMEM((dom, rows, long), b16),
        pltpu.VMEM((padded, BLOCK), f32),
        pltpu.VMEM((dom, padded, BLOCK), f32),
    ]
    for shape in ((dom,), (dom,), (cls,), (2, dom), (dom,)):
        scratch += [pltpu.SemaphoreType.DMA(shape)] * 2
    return pl.pallas_call(
        functools.partial(em_kernel, dom, cls, classes),
        out_shape=(
            jax.ShapeDtypeStruct((rows, long), f32),
            jax.ShapeDtypeStruct((padded, BLOCK), f32),
            jax.ShapeDtypeStruct((8, particle_count), f32),
        ),
        in_specs=[pl.BlockSpec(memory_space=pltpu.VMEM)] * 5,
        out_specs=(pl.BlockSpec(memory_space=pltpu.VMEM),) * 3,
        scratch_shapes=scratch,
        compiler_params=pltpu.CompilerParams(
            collective_id=0, has_side_effects=True, vmem_limit_bytes=40 * 1024 * 1024
        ),
    )(w, h, x, straight, crossed)


def per_device(dom, cls, particles, references, noise_weights):
    particle_count, _, angles, cycles = particles.shape
    classes = references.shape[0]
    cycle_count = cycles // dom
    rows = -(-cycle_count // 16) * 16
    padded = -(-classes // 8) * 8
    used = classes * 2 * angles
    long = -(-used // BLOCK) * BLOCK
    table = angular_table(angles)
    mine = jnp.arange(dom)[:, None] == lax.axis_index("dom")
    noise = jnp.sum(jnp.where(mine, noise_weights.reshape(dom, cycle_count), 0.0), axis=0)

    ref_spectra = jnp.einsum(
        "cpar,paqm->rmqc", references, table, preferred_element_type=jnp.float32
    )
    weighted = (noise[:, None, None, None] * ref_spectra).astype(jnp.bfloat16)
    weighted = jnp.pad(
        weighted.reshape(cycle_count, used), ((0, rows - cycle_count), (0, long - used))
    )
    own_wide = references.astype(jnp.float32)
    norms = jnp.sum(noise * own_wide * own_wide, axis=(1, 2, 3))
    norms = jnp.broadcast_to(jnp.pad(norms, (0, padded - classes))[:, None], (padded, BLOCK))
    arranged = jnp.transpose(particles, (2, 0, 1, 3)).reshape(angles, particle_count, 2 * cycles)
    straight, crossed = phase_constants(angles, cycles)
    own_sums, own_weights, evidence = em_step(
        dom, cls, classes, weighted, norms, arranged, straight, crossed
    )
    own_sums = own_sums[:cycle_count, :used].reshape(cycle_count, angles, 2, classes)
    own_sums = jnp.transpose(own_sums, (3, 2, 1, 0))
    denominator = noise * own_weights[:classes, 0:1] + ridge_term
    class_spectra = own_sums * (noise / denominator)[:, None, None, :]
    return (class_spectra, evidence[0])


def solution(mesh):
    dom, cls = mesh.shape["dom"], mesh.shape["cls"]
    return jax.shard_map(
        functools.partial(per_device, dom, cls),
        mesh=mesh,
        in_specs=(P("dom", None, None, None), P("cls", None, None, "dom"), P()),
        out_specs=(P("cls", None, None, "dom"), P("dom")),
        check_vma=False,
    )
```

```python
import functools

import jax
import jax.numpy as jnp
import ml_dtypes
import numpy as np
from jax import lax
from jax.experimental import pallas as pl
from jax.experimental.pallas import tpu as pltpu
from jax.sharding import PartitionSpec as P

SHIFTS = 5
MESH = pl.DeviceIdType.MESH

ridge_term = 0.5
shift_x = (0.0, 1.0, -1.0, 0.0, 0.0)
shift_y = (0.0, 0.0, 0.0, 1.0, -1.0)


def rotation_tables(angles):
    steps = jnp.arange(angles, dtype=jnp.int32)
    product = steps[:, None] * steps[None, :] % angles
    turn = 2.0 * jnp.pi * product.astype(jnp.float32) / angles
    return (jnp.cos(turn), jnp.sin(turn))


def angular_table(angles):
    cosine, sine = rotation_tables(angles)
    upper = jnp.stack([cosine, -sine], axis=1)
    lower = jnp.stack([sine, cosine], axis=1)
    return jnp.stack([upper, lower], axis=0).astype(jnp.bfloat16)


def greet(counts):
    barrier = pltpu.get_barrier_semaphore()
    for axis, count in counts.items():
        me = lax.axis_index(axis)
        for step in range(1, count):
            pl.semaphore_signal(
                barrier,
                inc=1,
                device_id={axis: lax.rem(me + step, count)},
                device_id_type=MESH,
            )
    pl.semaphore_wait(barrier, sum(counts.values()) - len(counts))


def push(axis, count, me, source, land, send_sem, recv_sem, lanes=None):
    copies = []
    for step in range(1, count):
        peer = lax.rem(me + step, count)
        copy = pltpu.make_async_remote_copy(
            src_ref=source(peer),
            dst_ref=land.at[me] if lanes is None else land.at[me, :, lanes],
            send_sem=send_sem.at[step],
            recv_sem=recv_sem.at[step],
            device_id={axis: peer},
            device_id_type=MESH,
        )
        copy.start()
        copies.append(copy)
    return copies


def phase_constants(angles, cycles):
    theta = (2.0 * np.pi * np.arange(angles) / angles).astype(np.float32)
    radius = (np.arange(cycles) / (2.0 * cycles)).astype(np.float32)
    straight, crossed = [], []
    for dx, dy in zip(shift_x, shift_y):
        along = dx * np.cos(theta) + dy * np.sin(theta)
        phase = -2.0 * np.pi * along[:, None] * radius[None, :]
        cosine, sine = np.cos(phase), np.sin(phase)
        straight.append(np.concatenate([cosine, cosine], axis=1))
        crossed.append(np.concatenate([-sine, sine], axis=1))
    return np.stack(straight).astype(np.float32), np.stack(crossed).astype(np.float32)


def odd_factor(count):
    return count // 4


def full_root(index, count):
    turn = 2.0 * np.pi * (index % count) / count
    return float(np.cos(turn)), float(np.sin(turn))


def rounded_root(index, count):
    turn = 2.0 * np.pi * (index % count) / count
    cosine, sine = np.float32(np.cos(turn)), np.float32(np.sin(turn))
    return float(cosine.astype(ml_dtypes.bfloat16)), float(sine.astype(ml_dtypes.bfloat16))


def swapped(z):
    half = z.shape[-1] // 2
    return jnp.concatenate([z[..., half:], z[..., :half]], axis=-1)


def turned(z, axis):
    low, high = jnp.split(z, 2, axis=axis)
    return jnp.concatenate([high, -low], axis=axis)


def transform(load, middle, store, angles, root, axis):
    odd = odd_factor(angles)
    inverse = pow(4, -1, odd)
    quarter = pow(odd, -1, 4)
    for second in range(odd):
        z = [load((odd * first + 4 * second) % angles) for first in range(4)]
        plus, minus = z[0] + z[2], z[0] - z[2]
        other, differ = z[1] + z[3], turned(z[1] - z[3], axis)
        middle[0, second] = plus + other
        middle[1, second] = minus + differ
        middle[2, second] = plus - other
        middle[3, second] = minus - differ
    for first in range(4):
        head = middle[first, 0]
        pairs = odd // 2
        even, uneven = [], []
        for j in range(1, pairs + 1):
            low, high = middle[first, j], middle[first, odd - j]
            even.append(low + high)
            uneven.append(turned(low - high, axis))
        total = head
        for part in even:
            total = total + part
        store((odd * quarter * first) % angles, total)
        for k in range(1, pairs + 1):
            real, imag = head, None
            for j in range(1, pairs + 1):
                cosine, sine = root(k * j, odd)
                real = real + cosine * even[j - 1]
                term = sine * uneven[j - 1]
                imag = term if imag is None else imag + term
            base = odd * quarter * first
            store((base + 4 * inverse * k) % angles, real + imag)
            store((base + 4 * inverse * (odd - k)) % angles, real - imag)


TILE = 16
BLOCK = 128


def em_kernel(
    dom, cls, classes,
    w_ref, h_ref, x_ref, c_ref, s_ref,
    o_ref, u_ref, e_ref,
    spectra, w_land, h_land, turned_w, middle, corr, wide_middle, scores, weights,
    stat, stat_land, sums, outgoing, land, total_block, total_land,
    w_send, w_recv, h_send, h_recv, stat_send, stat_recv, o_send, o_recv, t_send, t_recv,
):
    greet({"dom": dom, "cls": cls})
    me, column = lax.axis_index("dom"), lax.axis_index("cls")
    copies = push("dom", dom, me, lambda peer: w_ref, w_land, w_send, w_recv)
    copies += push("dom", dom, me, lambda peer: h_ref, h_land, h_send, h_recv)
    w_land[me] = w_ref[...]
    h_land[me] = h_ref[...]
    angles, particle_count, width = x_ref.shape
    cycles = width // 2
    cycle_count = cycles // dom
    tiles = particle_count // TILE
    padded = scores.shape[1]
    pairs = 2 * classes

    def step(index, carry):
        shift = index // tiles
        start = pl.multiple_of(lax.rem(index, tiles) * TILE, TILE)
        target = pl.multiple_of(index * TILE, TILE)

        def load(angle):
            z = x_ref[angle, pl.ds(start, TILE), :].astype(jnp.float32)
            straight = c_ref[shift, pl.ds(angle, 1), :]
            crossed = s_ref[shift, pl.ds(angle, 1), :]
            return z * straight + swapped(z) * crossed

        def store(frequency, value):
            spectra[frequency, pl.ds(target, TILE), :] = value.astype(spectra.dtype)

        transform(load, middle, store, angles, rounded_root, 1)
        return carry

    lax.fori_loop(0, SHIFTS * tiles, step, 0)

    for copy in copies:
        copy.wait()
    half_norms = h_land[0]
    for index in range(1, dom):
        half_norms = half_norms + h_land[index]
    row = lax.broadcasted_iota(jnp.int32, half_norms.shape, 0)
    half_norms = jnp.where(row < classes, 0.5 * half_norms, 1e30)[:, 0:1]
    for block in range(turned_w.shape[0] // BLOCK):
        lanes = slice(block * BLOCK, (block + 1) * BLOCK)
        piece = jnp.concatenate(
            [w_land[index][:, lanes].astype(jnp.float32)[:cycle_count] for index in range(dom)], axis=0
        )
        turned_w[lanes, :] = piece.T

    def correlate(m, carry):
        both = turned_w[pl.ds(pl.multiple_of(m * pairs, 8), pairs), :]
        gap = jnp.zeros((padded - classes, cycles), jnp.float32)
        real = jnp.concatenate([both[:classes], gap], axis=0)
        imag = jnp.concatenate([both[classes:], gap], axis=0)
        left = jnp.concatenate([real, imag], axis=0)
        right = jnp.concatenate([imag, -real], axis=0)
        stacked = jnp.concatenate([left, right], axis=1).astype(jnp.bfloat16)
        corr[m] = lax.dot_general(
            stacked, spectra[m], (((1,), (1,)), ((), ())), preferred_element_type=jnp.float32
        )
        return carry

    lax.fori_loop(0, angles, correlate, 0, unroll=12)

    def keep_score(k, value):
        scores[k] = value[:padded] * (1.0 / angles) - half_norms

    transform(lambda m: corr[m], wide_middle, keep_score, angles, full_root, 0)

    def fold(values, combine):
        parts = [
            values[:, index * particle_count : (index + 1) * particle_count] for index in range(SHIFTS)
        ]
        return functools.reduce(combine, parts)

    def spread(values):
        return jnp.concatenate([values] * SHIFTS, axis=1)

    highest = scores[0]
    for k in range(1, angles):
        highest = jnp.maximum(highest, scores[k])
    peak = fold(jnp.max(highest, axis=0, keepdims=True), jnp.maximum)
    wide_peak = spread(peak)

    def exponentiate(k, total):
        value = jnp.exp(scores[k] - wide_peak)
        scores[k] = value
        return total + value

    empty = jnp.zeros(scores.shape[1:], jnp.float32)
    class_total = lax.fori_loop(0, angles, exponentiate, empty, unroll=6)
    total = fold(jnp.sum(class_total, axis=0, keepdims=True), jnp.add)
    row = lax.broadcasted_iota(jnp.int32, stat.shape, 0)
    stat[...] = jnp.where(row == 0, peak, total)
    copies = push("cls", cls, column, lambda peer: stat, stat_land, stat_send, stat_recv)
    stat_land[column] = stat[...]
    for copy in copies:
        copy.wait()
    peaks = stat_land[0][0:1]
    for index in range(1, cls):
        peaks = jnp.maximum(peaks, stat_land[index][0:1])
    totals = jnp.zeros_like(peaks)
    for index in range(cls):
        part = stat_land[index]
        totals = totals + part[1:2] * jnp.exp(part[0:1] - peaks)
    scale = spread(jnp.exp(peak - peaks) / totals)
    e_ref[...] = jnp.broadcast_to(peaks + jnp.log(totals), e_ref.shape)
    weight = jnp.sum(class_total * scale, axis=1, keepdims=True)
    total_block[...] = jnp.broadcast_to(weight, total_block.shape)
    copies = push("dom", dom, me, lambda peer: total_block, total_land, t_send, t_recv)
    total_land[me] = total_block[...]

    def load_posterior(k):
        value = scores[k] * scale
        return jnp.concatenate([value, jnp.zeros_like(value)], axis=0)

    def keep_weight(m, value):
        weights[m] = jnp.concatenate([value[:padded], -value[padded:]], axis=0).astype(weights.dtype)

    transform(load_posterior, wide_middle, keep_weight, angles, full_root, 0)

    used = angles * pairs
    if sums.shape[0] > used:
        sums[used:] = jnp.zeros((sums.shape[0] - used, cycles), jnp.float32)

    def accumulate(m, carry):
        parts = jnp.dot(weights[m], spectra[m], preferred_element_type=jnp.float32)
        real = parts[:padded, :cycles] - parts[padded:, cycles:]
        imag = parts[:padded, cycles:] + parts[padded:, :cycles]
        sums[pl.ds(pl.multiple_of(m * pairs, 8), pairs), :] = jnp.concatenate(
            [real[:classes], imag[:classes]], axis=0
        )
        return carry

    rows, blocks = outgoing.shape[1], sums.shape[0] // BLOCK
    split = (blocks + 1) // 2
    ready = min(angles, -(-split * BLOCK // pairs))
    for part, (first, last, head, tail) in enumerate(
        ((0, ready, 0, split), (ready, angles, split, blocks))
    ):
        lax.fori_loop(first, last, accumulate, 0, unroll=12)
        for block in range(head, tail):
            lanes = slice(block * BLOCK, (block + 1) * BLOCK)
            piece = sums[lanes, :].T
            for index in range(dom):
                own = piece[index * cycle_count : (index + 1) * cycle_count]
                if rows > cycle_count:
                    gap = jnp.zeros((rows - cycle_count, BLOCK), jnp.float32)
                    own = jnp.concatenate([own, gap], axis=0)
                outgoing[index, :, lanes] = own.astype(outgoing.dtype)
        lanes = slice(head * BLOCK, tail * BLOCK)
        copies += push(
            "dom", dom, me, lambda peer: outgoing.at[peer, :, lanes], land,
            o_send.at[part], o_recv.at[part], lanes,
        )
    land[me] = outgoing[me]
    for copy in copies:
        copy.wait()
    result = land[0].astype(jnp.float32)
    weight = total_land[0]
    for index in range(1, dom):
        result = result + land[index].astype(jnp.float32)
        weight = weight + total_land[index]
    o_ref[...] = result
    u_ref[...] = weight


def em_step(dom, cls, classes, w, h, x, straight, crossed):
    angles, particle_count, width = x.shape
    cycles = width // 2
    rows, long = w.shape
    padded = h.shape[0]
    images = SHIFTS * particle_count
    odd = odd_factor(angles)
    f32, b16 = jnp.float32, jnp.bfloat16
    scratch = [
        pltpu.VMEM((angles, images, width), b16),
        pltpu.VMEM((dom, rows, long), b16),
        pltpu.VMEM((dom,) + h.shape, f32),
        pltpu.VMEM((long, cycles), f32),
        pltpu.VMEM((4, odd, TILE, width), f32),
        pltpu.VMEM((angles, 2 * padded, images), f32),
        pltpu.VMEM((4, odd, 2 * padded, images), f32),
        pltpu.VMEM((angles, padded, images), f32),
        pltpu.VMEM((angles, 2 * padded, images), b16),
        pltpu.VMEM((8, particle_count), f32),
        pltpu.VMEM((cls, 8, particle_count), f32),
        pltpu.VMEM((long, cycles), f32),
        pltpu.VMEM((dom, rows, long), b16),
        pltpu.VMEM((dom, rows, long), b16),
        pltpu.VMEM((padded, BLOCK), f32),
        pltpu.VMEM((dom, padded, BLOCK), f32),
    ]
    for shape in ((dom,), (dom,), (cls,), (2, dom), (dom,)):
        scratch += [pltpu.SemaphoreType.DMA(shape)] * 2
    return pl.pallas_call(
        functools.partial(em_kernel, dom, cls, classes),
        out_shape=(
            jax.ShapeDtypeStruct((rows, long), f32),
            jax.ShapeDtypeStruct((padded, BLOCK), f32),
            jax.ShapeDtypeStruct((8, particle_count), f32),
        ),
        in_specs=[pl.BlockSpec(memory_space=pltpu.VMEM)] * 5,
        out_specs=(pl.BlockSpec(memory_space=pltpu.VMEM),) * 3,
        scratch_shapes=scratch,
        compiler_params=pltpu.CompilerParams(
            collective_id=0, has_side_effects=True, vmem_limit_bytes=40 * 1024 * 1024
        ),
    )(w, h, x, straight, crossed)


def per_device(dom, cls, particles, references, noise_weights):
    particle_count, _, angles, cycles = particles.shape
    classes = references.shape[0]
    cycle_count = cycles // dom
    rows = -(-cycle_count // 16) * 16
    padded = -(-classes // 8) * 8
    used = classes * 2 * angles
    long = -(-used // BLOCK) * BLOCK
    table = angular_table(angles)
    mine = jnp.arange(dom)[:, None] == lax.axis_index("dom")
    noise = jnp.sum(jnp.where(mine, noise_weights.reshape(dom, cycle_count), 0.0), axis=0)

    ref_spectra = jnp.einsum(
        "cpar,paqm->rmqc", references, table, preferred_element_type=jnp.float32
    )
    weighted = (noise[:, None, None, None] * ref_spectra).astype(jnp.bfloat16)
    weighted = jnp.pad(
        weighted.reshape(cycle_count, used), ((0, rows - cycle_count), (0, long - used))
    )
    own_wide = references.astype(jnp.float32)
    norms = jnp.sum(noise * own_wide * own_wide, axis=(1, 2, 3))
    norms = jnp.broadcast_to(jnp.pad(norms, (0, padded - classes))[:, None], (padded, BLOCK))
    arranged = jnp.transpose(particles, (2, 0, 1, 3)).reshape(angles, particle_count, 2 * cycles)
    straight, crossed = phase_constants(angles, cycles)
    own_sums, own_weights, evidence = em_step(
        dom, cls, classes, weighted, norms, arranged, straight, crossed
    )
    own_sums = own_sums[:cycle_count, :used].reshape(cycle_count, angles, 2, classes)
    own_sums = jnp.transpose(own_sums, (3, 2, 1, 0))
    denominator = noise * own_weights[:classes, 0:1] + ridge_term
    class_spectra = own_sums * (noise / denominator)[:, None, None, :]
    return (class_spectra, evidence[0])


def solution(mesh):
    dom, cls = mesh.shape["dom"], mesh.shape["cls"]
    return jax.shard_map(
        functools.partial(per_device, dom, cls),
        mesh=mesh,
        in_specs=(P("dom", None, None, None), P("cls", None, None, "dom"), P()),
        out_specs=(P("cls", None, None, "dom"), P("dom")),
        check_vma=False,
    )
```
